256 devices in a mesh: blk: 64 (over z, x_lo, y), grp: 4 (over x_hi, core).
Axes of the slice: x: 4 (x_hi: 2, x_lo: 2; x = x_hi * 2 + x_lo), y: 4, z: 8, core: 2. Of those that a mesh axis runs over, the one named last changes fastest.
Arguments:
- queries: bfloat16 [49152, 1024], P('blk'), may hold values from -18 to 18
- passages: bfloat16 [393216, 1024], P(('blk', 'grp')), may hold values from -18 to 18
- loss_grad: float32 [49152], P('blk'), may hold values from -40 to 40
- teacher_logits: float32 [8, 49152], P(None, 'blk'), may hold values from -8 to 410
- passage_ids: int32 [8, 49152], P(None, 'blk'), may hold values from 0 to 393215, as said below
Outputs:
- query_grad: bfloat16 [49152, 1024], P(('blk', 'grp'))
- passage_grad: bfloat16 [393216, 1024], P(('blk', 'grp'))
The draws below stay inside these ranges and needn't reach their ends.
Inputs may be any that keep to these rules, and one draw needn't show every extreme that they name: passage_ids[0, i] names a passage of block i // 768, and every passage_ids[k, i] names a passage of block i // 768 or of block (i // 768 - 1) mod 64, where passage j lies in block j // 6144.
All inputs are finite; a program needn't handle non-finite values.
Results may differ from the reference program's by a relative error of at most 0.015.
Values may be sent and summed in bfloat16 or wider, within the bound.
No kernel may reach another device: no remote copies, remote signals or barrier semaphores. Data moves between devices by JAX's collectives and lax.ppermute only.
A program may use at most 128 MiB of HBM per device.

```python
import math
import jax
import jax.numpy as jnp
from jax import lax

D = 1024
CAND = 8
QDEV = 768
PASS_DEV = 1536
BLOCK_PASS = 6144
NBLK = 64
QUERIES = 49152
PASSAGES = 393216


def draw_queries(key, part):
    key = jax.random.fold_in(key, 1)
    keys = jax.random.split(key, 1)
    values = jnp.clip(jax.random.normal(keys[0], (QUERIES, D), jnp.float32), -3.5, 3.5)
    return jnp.clip(values, -18.0, 18.0).astype(jnp.bfloat16)


def draw_passages(key, part):
    key = jax.random.fold_in(key, 2)
    keys = jax.random.split(key, 1)
    nblk = QUERIES // QDEV
    ngrp = BLOCK_PASS // PASS_DEV
    values = jnp.clip(jax.random.normal(keys[0], (nblk, ngrp, PASS_DEV, D), jnp.float32), -3.5, 3.5)
    level = jnp.arange(ngrp, dtype=jnp.float32).reshape(1, ngrp, 1, 1) / max(ngrp - 1, 1)
    values = values * (0.85 + 0.3 * level)
    return jnp.clip(values, -18.0, 18.0).reshape(PASSAGES, D).astype(jnp.bfloat16)


def draw_teacher_logits(key, part):
    key = jax.random.fold_in(key, 3)
    keys = jax.random.split(key, 1)
    values = jnp.clip(2.0 * jax.random.normal(keys[0], (CAND, QUERIES), jnp.float32), -8.0, 8.0)
    return values


def draw_passage_ids(key, part):
    key = jax.random.fold_in(key, 4)
    keys = jax.random.split(key, 3)
    nblk = QUERIES // QDEV
    ngrp = BLOCK_PASS // PASS_DEV
    owner = (jnp.arange(QUERIES, dtype=jnp.int32) // QDEV).reshape(1, QUERIES)
    backward = jax.random.randint(keys[0], (CAND, QUERIES), 0, 2)
    backward = backward.at[0, :].set(0)
    chosen_block = (owner - backward + nblk) % nblk
    group_pick = jax.random.randint(keys[1], (CAND, QUERIES), 0, ngrp)
    row_pick = jax.random.randint(keys[2], (CAND, QUERIES), 0, PASS_DEV)
    chosen = (chosen_block * ngrp + group_pick) * PASS_DEV + row_pick
    chosen = chosen.at[1, 0].set(0).at[1, QUERIES - 1].set(PASSAGES - 1)
    return chosen.astype(jnp.int32)


def block_levels(own_key, dims, shards, smallest, high):
    level, own = 1.0, jax.random.fold_in(own_key, 6)
    for position, blocks in shards:
        heights = jnp.exp(jax.random.uniform(jax.random.fold_in(own, position), (blocks,), jnp.float32, smallest / len(shards), high / len(shards)))
        level = level * jnp.repeat(heights, dims[position] // blocks).reshape([-1 if axis == position else 1 for axis in range(len(dims))])
    return level


def gaussian(rng, shape, deviation, bound, cuts=(), kind=jnp.bfloat16):
    entries = jax.random.normal(rng, shape, jnp.float32) * deviation
    if len(cuts) > 0:
        entries = block_levels(rng, shape, cuts, -0.22, 0.18) * entries
    return jnp.clip(entries, min=-bound, max=bound).astype(kind)


def setup_inputs(seed: int = 0) -> dict:
    key_list = jax.random.split(jax.random.key(seed), 6)
    queries = draw_queries(jax.random.fold_in(key_list[5], 71), 0)
    passages = draw_passages(jax.random.fold_in(key_list[5], 71), 0)
    loss_grad = gaussian(key_list[2], (QUERIES,), 8.0, 40.0, ((0, 64),), jnp.float32)
    teacher_logits = draw_teacher_logits(jax.random.fold_in(key_list[5], 71), 0)
    passage_ids = draw_passage_ids(jax.random.fold_in(key_list[5], 71), 0)
    return {"queries": queries, "passages": passages, "loss_grad": loss_grad, "teacher_logits": teacher_logits, "passage_ids": passage_ids}


def contract(left_rows, right_rows):
    return lax.dot_general(left_rows, right_rows, (((1,), (1,)), ((), ())), preferred_element_type=jnp.float32)

def grad_product(grads, rows):
    return lax.dot_general(grads, rows, (((0,), (0,)), ((), ())), preferred_element_type=jnp.float32)

def reference(queries, passages, loss_grad, teacher_logits, passage_ids):
    score_scale = 3.0 / math.sqrt(D)
    query_coef = score_scale * loss_grad
    teacher_prob = jax.nn.softmax(teacher_logits, axis=0)
    weighted = query_coef[None, :] * teacher_prob
    passage_blocks = passages.reshape(NBLK, BLOCK_PASS, D)
    local_cols = lax.broadcasted_iota(jnp.int32, (BLOCK_PASS,), 0)

    def one_block(carry, blk_index):
        own_last, prev_first = carry
        earlier = (blk_index - 1 + NBLK) % NBLK
        start = (blk_index * QDEV).astype(jnp.int32)
        query_rows = lax.dynamic_slice_in_dim(queries, start, QDEV, 0)
        coef_rows = lax.dynamic_slice_in_dim(query_coef, start, QDEV, 0)
        weight_rows = lax.dynamic_slice_in_dim(weighted, start, QDEV, 1)
        id_rows = lax.dynamic_slice_in_dim(passage_ids, start, QDEV, 1)
        own_block = lax.dynamic_index_in_dim(passage_blocks, blk_index, 0, keepdims=False)
        prev_block = lax.dynamic_index_in_dim(passage_blocks, earlier, 0, keepdims=False)
        window = jnp.concatenate((own_block, prev_block), axis=0)
        columns = jnp.concatenate((blk_index * BLOCK_PASS + local_cols, earlier * BLOCK_PASS + local_cols)).astype(jnp.int32)
        scores = score_scale * contract(query_rows, window)
        row_lse = jax.nn.logsumexp(scores, axis=1)
        target = jnp.zeros(scores.shape, jnp.float32)
        for cand_slot in range(CAND):
            target = target + jnp.where(id_rows[cand_slot][:, None] == columns[None, :], weight_rows[cand_slot][:, None], 0.0)
        score_grad = (coef_rows[:, None] * jnp.exp(scores - row_lse[:, None]) - target).astype(jnp.bfloat16)
        query_part = jnp.dot(score_grad, window, preferred_element_type=jnp.float32).astype(jnp.bfloat16)
        own_part = grad_product(score_grad[:, :BLOCK_PASS], query_rows)
        next_part = grad_product(score_grad[:, BLOCK_PASS:], query_rows).astype(jnp.bfloat16)
        next_wide = lax.optimization_barrier(next_part).astype(jnp.float32)
        out_block = (own_last + next_wide).astype(jnp.bfloat16)
        kept_first = jnp.where(blk_index == 0, next_part, prev_first)
        return ((own_part, kept_first), (query_part, out_block))
    start_carry = (jnp.zeros((BLOCK_PASS, D), jnp.float32), jnp.zeros((BLOCK_PASS, D), jnp.bfloat16))
    final_carry, outputs = lax.scan(one_block, start_carry, jnp.arange(NBLK, dtype=jnp.int32))
    query_parts, out_blocks = outputs
    own_final, first_next = final_carry
    last_block = (own_final + lax.optimization_barrier(first_next).astype(jnp.float32)).astype(jnp.bfloat16)
    passage_grad = jnp.concatenate((out_blocks[1:], last_block[None]), axis=0).reshape(PASSAGES, D)
    query_grad = query_parts.reshape(QUERIES, D)
    return (query_grad, passage_grad)
```

```python
import functools
import math

import jax
import jax.numpy as jnp
from jax import lax
from jax.experimental import pallas as pl
from jax.experimental.pallas import tpu as pltpu
from jax.sharding import PartitionSpec as P

AXES = ("blk", "grp")
LANE = 128
LOG2E = 1.4426950408889634
IN_VMEM = pl.BlockSpec(memory_space=pltpu.VMEM)
TILE = 256
ROWS = 64


def shape(dims, dtype):
    return jax.ShapeDtypeStruct(dims, dtype)


def eye(rows, cols):
    return (
        lax.broadcasted_iota(jnp.int32, (rows, cols), 0)
        == lax.broadcasted_iota(jnp.int32, (rows, cols), 1)
    )


def lanes_of(column, out, row, quarter):
    for at in range(0, quarter, LANE):
        width = min(LANE, quarter - at)
        piece = jnp.broadcast_to(column[at : at + width], (width, LANE))
        out[row : row + 1, at : at + LANE] = jnp.sum(
            jnp.where(eye(width, LANE), piece, 0.0), axis=0, keepdims=True
        )


def column_of(line, quarter):
    parts = []
    for at in range(0, quarter, LANE):
        width = min(LANE, quarter - at)
        piece = jnp.broadcast_to(line[:, at : at + LANE], (width, LANE))
        parts.append(jnp.sum(jnp.where(eye(width, LANE), piece, 0.0), axis=1, keepdims=True))
    return jnp.concatenate(parts, axis=0)


def fill_scores(scale, rows_ref, pass_ref, scores_ref, top_ref):
    top_ref[...] = jnp.full(top_ref.shape, -jnp.inf, jnp.float32)

    def step(tile, carry):
        at = pl.multiple_of(tile * TILE, TILE)
        scores = scale * lax.dot_general(
            rows_ref[...],
            pass_ref[pl.ds(at, TILE), :],
            (((1,), (1,)), ((), ())),
            preferred_element_type=jnp.float32,
        )
        scores_ref[:, pl.ds(at, TILE)] = scores
        best = top_ref[...]
        for lane in range(0, TILE, LANE):
            best = jnp.maximum(best, scores[:, lane : lane + LANE])
        top_ref[...] = best
        return carry

    lax.fori_loop(0, pass_ref.shape[0] // TILE, step, 0)


def exponentials(scores_ref, top_ref, total_ref, floor_ref=None):
    width = scores_ref.shape[1]

    def step(block, carry):
        rows = pl.ds(pl.multiple_of(block * ROWS, ROWS), ROWS)
        top = jnp.max(top_ref[rows, :], axis=1, keepdims=True)
        if floor_ref is not None:
            top = jnp.maximum(top, floor_ref[rows, :1])
        total = jnp.zeros((ROWS, LANE), jnp.float32)
        for at in range(0, width, LANE):
            value = jnp.exp2(scores_ref[rows, at : at + LANE] - top)
            scores_ref[rows, at : at + LANE] = value
            total = total + value
        top_ref[rows, :] = jnp.broadcast_to(top, (ROWS, LANE))
        total_ref[rows, :] = jnp.broadcast_to(
            jnp.sum(total, axis=1, keepdims=True), (ROWS, LANE)
        )
        return carry

    lax.fori_loop(0, scores_ref.shape[0] // ROWS, step, 0)


def own_kernel(scale, q_ref, p_ref, exp_ref, stat_ref, slot_ref, top_ref, total_ref):
    quarter = q_ref.shape[0] // 4
    group = lax.axis_index("grp")
    for slot in range(4):
        first = pl.multiple_of((group ^ slot) * quarter, quarter)
        slot_ref[slot * quarter : (slot + 1) * quarter, :] = q_ref[pl.ds(first, quarter), :]
    fill_scores(scale, slot_ref, p_ref, exp_ref, top_ref)
    exponentials(exp_ref, top_ref, total_ref)
    stat_ref[...] = jnp.zeros(stat_ref.shape, jnp.float32)
    for slot in range(4):
        rows = slice(slot * quarter, (slot + 1) * quarter)
        lanes_of(top_ref[rows, :1], stat_ref, slot, quarter)
        lanes_of(total_ref[rows, :1], stat_ref, 4 + slot, quarter)


def next_kernel(scale, slots, mine_ref, other_ref, p_ref, before_ref, *rest):
    known_ref = rest[0] if len(rest) == 7 else None
    exp_ref, stat_ref, rows_ref, top_ref, total_ref, floor_ref = rest[-6:]
    quarter = mine_ref.shape[0]
    rows_ref[:quarter, :] = mine_ref[...]
    rows_ref[quarter:, :] = other_ref[...]
    fill_scores(scale, rows_ref, p_ref, exp_ref, top_ref)
    for place, slot in enumerate(slots):
        floor_ref[place * quarter : (place + 1) * quarter, :] = jnp.broadcast_to(
            column_of(before_ref[slot : slot + 1, :], quarter), (quarter, LANE)
        )
    exponentials(exp_ref, top_ref, total_ref, floor_ref)
    if known_ref is None:
        stat_ref[...] = jnp.zeros(stat_ref.shape, jnp.float32)
    else:
        stat_ref[...] = known_ref[...]
    for place, slot in enumerate(slots):
        rows = slice(place * quarter, (place + 1) * quarter)
        lanes_of(top_ref[rows, :1], stat_ref, slot, quarter)
        lanes_of(total_ref[rows, :1], stat_ref, 4 + slot, quarter)
        stat_ref[4 + slot : 5 + slot, :] += before_ref[4 + slot : 5 + slot, :] * jnp.exp2(
            before_ref[slot : slot + 1, :] - stat_ref[slot : slot + 1, :]
        )


def target_kernel(quarter, pack_ref, target_ref):
    width = target_ref.shape[1]
    group = lax.axis_index("grp")
    steps = quarter // 32
    lane = lax.broadcasted_iota(jnp.int32, (32, LANE), 1).astype(jnp.float32)

    def step(block, carry):
        slot, inner = block // steps, block % steps
        source = pl.multiple_of((group ^ slot) * quarter + inner * 32, 32)
        pack = pack_ref[pl.ds(source, 32), :]
        ids = [jnp.broadcast_to(pack[:, k : k + 1], (32, LANE)) for k in range(8)]
        weights = [jnp.broadcast_to(pack[:, 8 + k : 9 + k], (32, LANE)) for k in range(8)]
        rows = pl.ds(pl.multiple_of(block * 32, 32), 32)
        for at in range(0, width, LANE):
            column = lane + float(at)
            value = jnp.zeros((32, LANE), jnp.float32)
            for k in range(8):
                value = jnp.where(ids[k] == column, weights[k], value)
            target_ref[rows, at : at + LANE] = value
        return carry

    lax.fori_loop(0, 4 * steps, step, 0)


def merge_stats(stat_ref, cross_ref, core_ref, both_ref, whole_ref):
    for slot in range(4):
        pairs = []
        for ref, turn in ((stat_ref, 0), (core_ref, 1), (cross_ref, 2), (both_ref, 3)):
            at = slot ^ turn
            pairs.append((ref[at : at + 1, :], ref[4 + at : 5 + at, :]))
        top = functools.reduce(jnp.maximum, [pair[0] for pair in pairs])
        total = sum(pair[1] * jnp.exp2(pair[0] - top) for pair in pairs)
        whole_ref[slot : slot + 1, :] = top
        whole_ref[4 + slot : 5 + slot, :] = total


def grad_kernel(slots, first_row, merge, *refs):
    if merge:
        exp_ref, target_ref, pack_ref, p_ref, stat_ref, cross_ref, core_ref, both_ref = refs[:8]
        grad_ref, mine_ref, other_ref, whole_ref, factor_ref = refs[8:]
        merge_stats(stat_ref, cross_ref, core_ref, both_ref, whole_ref)
    else:
        exp_ref, target_ref, pack_ref, p_ref, stat_ref, whole_ref = refs[:6]
        grad_ref, mine_ref, other_ref, factor_ref = refs[6:]
    quarter = mine_ref.shape[0]
    width = grad_ref.shape[1]
    group = lax.axis_index("grp")
    for place, slot in enumerate(slots):
        line = jnp.exp2(stat_ref[slot : slot + 1, :] - whole_ref[slot : slot + 1, :])
        line = line / whole_ref[4 + slot : 5 + slot, :]
        source = pl.multiple_of((group ^ slot) * quarter, quarter)
        factor = column_of(line, quarter) * pack_ref[pl.ds(source, quarter), 16:17]
        factor_ref[place * quarter : (place + 1) * quarter, :] = jnp.broadcast_to(
            factor, (quarter, LANE)
        )

    offset = first_row[0], first_row[1]

    def step(block, carry):
        at = pl.multiple_of(block * 32, 32)
        rows = pl.ds(at, 32)
        exp_rows = pl.ds(pl.multiple_of(at + offset[0], 32), 32)
        target_rows = pl.ds(pl.multiple_of(at + offset[1], 32), 32)
        factor = factor_ref[rows, :]
        for lane in range(0, width, LANE):
            grad_ref[rows, lane : lane + LANE] = (
                factor * exp_ref[exp_rows, lane : lane + LANE]
                - target_ref[target_rows, lane : lane + LANE]
            ).astype(jnp.bfloat16)
        return carry

    lax.fori_loop(0, grad_ref.shape[0] // 32, step, 0)
    for at in range(0, p_ref.shape[1], TILE):
        part = jnp.dot(
            grad_ref[...], p_ref[:, at : at + TILE], preferred_element_type=jnp.float32
        ).astype(jnp.bfloat16)
        mine_ref[:, at : at + TILE] = part[:quarter]
        other_ref[:, at : at + TILE] = part[quarter:]


def passage_kernel(count, *refs):
    grads, rows, out_ref = refs[:count], refs[count : 2 * count], refs[2 * count]

    def step(tile, carry):
        at = pl.multiple_of(tile * TILE, TILE)
        total = None
        for grad_ref, rows_ref in zip(grads, rows):
            part = lax.dot_general(
                grad_ref[:, pl.ds(at, TILE)],
                rows_ref[...],
                (((0,), (0,)), ((), ())),
                preferred_element_type=jnp.float32,
            )
            total = part if total is None else total + part
        out_ref[pl.ds(at, TILE), :] = total.astype(jnp.bfloat16)
        return carry

    lax.fori_loop(0, out_ref.shape[0] // TILE, step, 0)


def call(kernel, outs, ins, scratch=(), flops=0, name=None):
    size = sum(math.prod(o.shape) * o.dtype.itemsize for o in list(outs) + list(ins))
    return pl.pallas_call(
        kernel,
        out_shape=tuple(outs),
        in_specs=[IN_VMEM] * len(ins),
        out_specs=(IN_VMEM,) * len(outs),
        scratch_shapes=list(scratch),
        compiler_params=pltpu.CompilerParams(vmem_limit_bytes=16 * 2**20),
        cost_estimate=pl.CostEstimate(
            flops=int(flops), bytes_accessed=int(size), transcendentals=0
        ),
        name=name,
    )(*ins)


def per_device(queries, passages, loss_grad, teacher_logits, passage_ids):
    rows, depth = queries.shape
    width = passages.shape[0]
    quarter, half = rows // 4, rows // 2
    blocks, groups = lax.axis_size("blk"), lax.axis_size("grp")
    blk_index, grp_index = lax.axis_index("blk"), lax.axis_index("grp")
    f32, bf16 = jnp.float32, jnp.bfloat16
    score_scale = 3.0 / math.sqrt(depth)

    def along(by):
        return [
            (b * groups + g, (b + by) % blocks * groups + g)
            for b in range(blocks)
            for g in range(groups)
        ]

    def across(turn):
        return [
            (b * groups + g, b * groups + (g ^ turn))
            for b in range(blocks)
            for g in range(groups)
        ]

    def move(x, pairs):
        return lax.ppermute(x, AXES, pairs)

    def quarter_rows(slot):
        first = (grp_index ^ slot) * quarter
        return lax.dynamic_slice_in_dim(queries, first, quarter, 0)

    a_mine = move(quarter_rows(0), along(-1))
    b_mine = move(quarter_rows(2), along(-1))

    coef = score_scale * loss_grad
    weighted = coef[None, :] * jax.nn.softmax(teacher_logits, axis=0)
    same = passage_ids[:, None, :] == passage_ids[None, :, :]
    weighted = jnp.sum(jnp.where(same, weighted[None], 0.0), axis=1)

    def packed(block):
        first = (block * groups + grp_index) * width
        return jnp.concatenate(
            [
                (passage_ids - first).astype(f32),
                weighted,
                jnp.broadcast_to(coef[None, :], (8, rows)),
            ]
        )

    pack_next = move(packed((blk_index - 1 + blocks) % blocks), along(-1)).T
    pack_own = packed(blk_index).T

    a_other = move(a_mine, across(1))
    b_other = move(b_mine, across(1))

    scale = score_scale * LOG2E
    stat = shape((8, 2 * LANE), f32)
    exp_own, stat_own, q_slots = call(
        functools.partial(own_kernel, scale),
        [shape((rows, width), f32), stat, shape((rows, depth), bf16)],
        [queries, passages],
        [pltpu.VMEM((rows, LANE), f32)] * 2,
        flops=2 * rows * width * depth,
        name="own_scores",
    )
    stat_before = move(stat_own, along(-1))
    (target_own,) = call(
        functools.partial(target_kernel, quarter), [shape((rows, width), f32)], [pack_own],
        flops=rows * width * 1500, name="own_target",
    )
    (target_next,) = call(
        functools.partial(target_kernel, quarter), [shape((rows, width), f32)], [pack_next],
        flops=rows * width * 1500, name="next_target",
    )

    def next_scores(slots, mine, other, known, name):
        return call(
            functools.partial(next_kernel, scale, slots),
            [shape((half, width), f32), stat, shape((half, depth), bf16)],
            [mine, other, passages, stat_before] + known,
            [pltpu.VMEM((half, LANE), f32)] * 3,
            flops=2 * half * width * depth,
            name=name,
        )

    exp_a, stat_a, q_a = next_scores((0, 1), a_mine, a_other, [], "next_scores_a")
    exp_b, stat_next, q_b = next_scores((2, 3), b_mine, b_other, [stat_a], "next_scores_b")

    cross, core, both = (move(stat_next, across(turn)) for turn in (2, 1, 3))

    def grads(slots, offsets, exps, target, pack, stats, merge, name):
        outs = [shape((half, width), bf16)] + [shape((quarter, depth), bf16)] * 2
        return call(
            functools.partial(grad_kernel, slots, offsets, merge),
            outs + ([stat] if merge else []),
            [exps, target, pack, passages] + stats,
            [pltpu.VMEM((half, LANE), f32)],
            flops=2 * half * width * depth,
            name=name,
        )

    g_b, nb_mine, nb_other, whole_next = grads(
        (2, 3), (0, half), exp_b, target_next, pack_next, [stat_next, cross, core, both], True,
        "next_grad_b",
    )
    whole_own = move(whole_next, along(1))
    nb = (nb_mine.astype(f32) + move(nb_other, across(1)).astype(f32)).astype(bf16)
    nb_in = move(nb, across(2))
    g_a, na_mine, na_other = grads(
        (0, 1), (0, 0), exp_a, target_next, pack_next, [stat_next, whole_next], False,
        "next_grad_a",
    )
    na_in = move(na_other, across(1))
    g_ob, ob_mine, ob_other = grads(
        (2, 3), (half, half), exp_own, target_own, pack_own, [stat_own, whole_own], False,
        "own_grad_b",
    )
    ob = (ob_mine.astype(f32) + move(ob_other, across(1)).astype(f32)).astype(bf16)
    ob_in = move(ob, across(2))
    g_oa, oa_mine, oa_other = grads(
        (0, 1), (0, 0), exp_own, target_own, pack_own, [stat_own, whole_own], False,
        "own_grad_a",
    )
    oa_in = move(oa_other, across(1))
    sent = (na_mine.astype(f32) + na_in.astype(f32) + nb_in.astype(f32)).astype(bf16)
    came = move(sent, along(1))
    (passage_grad,) = call(
        functools.partial(passage_kernel, 4),
        [shape((width, depth), bf16)],
        [g_b, g_a, g_ob, g_oa, q_b, q_a, q_slots[half:], q_slots[:half]],
        flops=4 * rows * width * depth,
        name="passage_grad",
    )
    query_grad = (
        oa_mine.astype(f32) + oa_in.astype(f32) + ob_in.astype(f32) + came.astype(f32)
    ).astype(bf16)
    return query_grad, passage_grad


def solution(mesh):
    in_specs = (P("blk", None), P(("blk", "grp"), None), P("blk"), P(None, "blk"), P(None, "blk"))
    out_specs = (P(("blk", "grp"), None), P(("blk", "grp"), None))
    return jax.shard_map(
        per_device, mesh=mesh, in_specs=in_specs, out_specs=out_specs, check_vma=False
    )
```

```python
import functools
import math

import jax
import jax.numpy as jnp
from jax import lax
from jax.experimental import pallas as pl
from jax.experimental.pallas import tpu as pltpu
from jax.sharding import PartitionSpec as P

AXES = ("blk", "grp")
LANE = 128
LOG2E = 1.4426950408889634
IN_VMEM = pl.BlockSpec(memory_space=pltpu.VMEM)
TILE = 256
ROWS = 64
FEW = 4


def shape(dims, dtype):
    return jax.ShapeDtypeStruct(dims, dtype)


def reorder(x, group):
    half = x.shape[1] // 2
    parts = [x[:, :half], x[:, half:]]
    parts = [jnp.where(group % 2 == 1, pltpu.roll(part, half // 2, 1), part) for part in parts]
    swap = group >= 2
    return jnp.concatenate(
        [jnp.where(swap, parts[1], parts[0]), jnp.where(swap, parts[0], parts[1])], axis=1
    )


def fill_scores(scale, p_ref, q_ref, out_ref):
    for at in range(0, q_ref.shape[0], TILE):
        to = min(at + TILE, q_ref.shape[0])
        out_ref[:, at:to] = scale * lax.dot_general(
            p_ref[...], q_ref[at:to, :], (((1,), (1,)), ((), ())),
            preferred_element_type=jnp.float32,
        )


def exponentials(ref, floor=None):
    rows, cols = ref.shape
    fold = (ROWS // 8, 8, cols)

    def find(block, top):
        at = pl.multiple_of(block * ROWS, ROWS)
        return jnp.maximum(top, jnp.max(ref[pl.ds(at, ROWS), :].reshape(fold), axis=0))

    top = lax.fori_loop(0, rows // ROWS, find, jnp.full((8, cols), -jnp.inf, jnp.float32))
    top = jnp.max(top, axis=0, keepdims=True)
    if floor is not None:
        top = jnp.maximum(top, floor)

    def raised(block, total):
        at = pl.multiple_of(block * ROWS, ROWS)
        value = jnp.exp2(ref[pl.ds(at, ROWS), :] - top)
        ref[pl.ds(at, ROWS), :] = value
        return total + jnp.sum(value.reshape(fold), axis=0)

    total = lax.fori_loop(0, rows // ROWS, raised, jnp.zeros((8, cols), jnp.float32))
    return top, jnp.sum(total, axis=0, keepdims=True)


def own_kernel(scale, q_ref, p_ref, exp_ref, stat_ref):
    fill_scores(scale, p_ref, q_ref, exp_ref)
    top, total = exponentials(exp_ref)
    stat_ref[0:1, :] = top
    stat_ref[1:2, :] = total


def next_kernel(scale, *refs):
    pieces, p_ref, before_ref, exp_ref, stat_ref, rows_ref = refs[:6], *refs[6:]
    first_mine, first_other, cross_mine, cross_other, rest_mine, rest_other = pieces
    cut, left = first_mine.shape[0], rest_mine.shape[0] // 2
    at = 0
    for lead, rest, skip in (
        (first_mine, rest_mine, 0),
        (first_other, rest_other, 0),
        (cross_mine, rest_mine, left),
        (cross_other, rest_other, left),
    ):
        rows_ref[at : at + cut, :] = lead[...]
        rows_ref[at + cut : at + cut + left, :] = rest[skip : skip + left, :]
        at += cut + left
    fill_scores(scale, p_ref, rows_ref, exp_ref)
    before = reorder(before_ref[...], lax.axis_index("grp"))
    top, total = exponentials(exp_ref, before[0:1])
    stat_ref[0:1, :] = top
    stat_ref[1:2, :] = total + before[1:2] * jnp.exp2(before[0:1] - top)


def pack_kernel(width, ids_ref, logits_ref, coef_ref, own_ref, next_ref):
    device = lax.axis_index("blk") * 4 + lax.axis_index("grp")
    blocks = lax.axis_size("blk")
    before = (lax.axis_index("blk") + blocks - 1) % blocks * 4 + lax.axis_index("grp")
    ids = ids_ref[...]
    logits = logits_ref[...]
    power = jnp.exp(logits - jnp.max(logits, axis=0, keepdims=True))
    weights = coef_ref[...] * (power / jnp.sum(power, axis=0, keepdims=True))
    summed = jnp.zeros_like(weights)
    for k in range(8):
        summed = summed + jnp.where(ids == ids[k : k + 1], weights[k : k + 1], 0.0)
    for ref, at in ((own_ref, device), (next_ref, before)):
        place = ids - at * width
        inside = (place >= 0) & (place < width)
        places, count = [-1.0] * 8, jnp.zeros_like(coef_ref[...])
        values = [0.0] * 8
        for k in range(8):
            here = inside[k : k + 1]
            for r in range(k + 1):
                chosen = here & (count == r)
                places[r] = jnp.where(chosen, place[k : k + 1].astype(jnp.float32), places[r])
                values[r] = jnp.where(chosen, summed[k : k + 1], values[r])
            count = count + here.astype(jnp.float32)
        for r in range(8):
            ref[r : r + 1, :] = places[r]
            ref[8 + r : 9 + r, :] = values[r]
        ref[16:24, :] = jnp.broadcast_to(coef_ref[...], ids.shape)


def merge_stats(stat, cross, core, both):
    half = stat.shape[1] // 2
    quarter = half // 2

    def turned(x):
        return jnp.concatenate(
            [pltpu.roll(x[:, :half], quarter, 1), pltpu.roll(x[:, half:], quarter, 1)], axis=1
        )

    def crossed(x):
        return jnp.concatenate([x[:, half:], x[:, :half]], axis=1)

    parts = (stat, turned(core), crossed(cross), crossed(turned(both)))
    top = functools.reduce(jnp.maximum, [part[0:1] for part in parts])
    return top, sum(part[1:2] * jnp.exp2(part[0:1] - top) for part in parts)


def fill_grads(exp_ref, grad_ref, factor, ids, weights):
    rows, cols = exp_ref.shape
    lead = lax.broadcasted_iota(jnp.int32, (16, cols), 0)

    def fill(count):
        def step(block, carry):
            at = pl.multiple_of(block * 16, 16)
            place = (lead + block * 16).astype(jnp.float32)
            value = jnp.zeros((16, cols), jnp.float32)
            for k in range(count):
                value = jnp.where(ids[k : k + 1] == place, weights[k : k + 1], value)
            grad_ref[pl.ds(at, 16), :] = (factor * exp_ref[pl.ds(at, 16), :] - value).astype(
                jnp.bfloat16
            )
            return carry

        return step

    lax.fori_loop(0, rows // 16, fill(FEW), 0)
    more = ids[FEW:]
    low = jnp.min(jnp.where(more >= 0, more, float(rows))).astype(jnp.int32)
    high = jnp.max(more).astype(jnp.int32)
    lax.fori_loop(low // 16, jnp.where(high >= 0, high // 16 + 1, 0), fill(8), 0)


def query_product(grad_ref, p_ref, out):
    for at in range(0, p_ref.shape[1], TILE):
        out(
            at,
            lax.dot_general(
                grad_ref[...], p_ref[:, at : at + TILE], (((0,), (0,)), ((), ())),
                preferred_element_type=jnp.float32,
            ).astype(jnp.bfloat16),
        )


def next_grad_kernel(place, merge, exp_ref, pack_ref, p_ref, stat_ref, *refs):
    group = lax.axis_index("grp")
    if merge:
        cross_ref, core_ref, both_ref, grad_ref, mine_ref, other_ref, whole_ref = refs
        top, total = merge_stats(stat_ref[...], cross_ref[...], core_ref[...], both_ref[...])
        whole_ref[0:1, :] = top
        whole_ref[1:2, :] = total
    else:
        whole_ref, grad_ref, mine_ref, other_ref = refs
        top, total = whole_ref[0:1, :], whole_ref[1:2, :]
    quarter = mine_ref.shape[0]
    lanes = slice(place * 2 * quarter, (place + 1) * 2 * quarter)
    pack = reorder(pack_ref[...], group)[:, lanes]
    factor = pack[16:17] * (jnp.exp2(stat_ref[0:1, lanes] - top[:, lanes]) / total[:, lanes])
    fill_grads(exp_ref.at[:, lanes], grad_ref, factor, pack[0:8], pack[8:16])

    def put(at, part):
        mine_ref[:, at : at + TILE] = part[:quarter]
        other_ref[:, at : at + TILE] = part[quarter:]

    query_product(grad_ref, p_ref, put)


def own_grad_kernel(exp_ref, pack_ref, p_ref, stat_ref, whole_ref, grad_ref, *outs):
    *outs, rows_ref = outs
    group = lax.axis_index("grp")
    whole = reorder(whole_ref[...], group)
    factor = pack_ref[16:17, :] * (jnp.exp2(stat_ref[0:1, :] - whole[0:1]) / whole[1:2])
    fill_grads(exp_ref, grad_ref, factor, pack_ref[0:8, :], pack_ref[8:16, :])

    def put(at, part):
        rows_ref[:, at : at + TILE] = part

    query_product(grad_ref, p_ref, put)
    quarter = outs[0].shape[0]
    for slot in range(4):
        first = pl.multiple_of((group ^ slot) * quarter, quarter)
        outs[slot][...] = rows_ref[pl.ds(first, quarter), :]


def passage_kernel(count, half, *refs):
    grads, (rows_ref, next_ref, out_ref) = refs[:count], refs[count:]
    rows = (rows_ref, next_ref.at[half:, :], next_ref.at[:half, :])
    for at in range(0, out_ref.shape[1], TILE):
        out_ref[:, at : at + TILE] = sum(
            jnp.dot(
                grad_ref[...], rows_ref[:, at : at + TILE], preferred_element_type=jnp.float32
            )
            for grad_ref, rows_ref in zip(grads, rows)
        ).astype(jnp.bfloat16)


def take_kernel(pieces, q_ref, out_ref, sems):
    quarter = q_ref.shape[0] // 4
    group = lax.axis_index("grp")
    copies, at = [], 0
    for place, (slot, skip, rows) in enumerate(pieces):
        first = pl.multiple_of((group ^ slot) * quarter + skip, 16)
        copies.append(
            pltpu.make_async_copy(
                q_ref.at[pl.ds(first, rows)], out_ref.at[pl.ds(at, rows)], sems.at[place]
            )
        )
        at += rows
    for copy in copies:
        copy.start()
    for copy in copies:
        copy.wait()


def call(kernel, outs, ins, scratch=(), flops=0, name=None):
    size = sum(math.prod(o.shape) * o.dtype.itemsize for o in list(outs) + list(ins))
    return pl.pallas_call(
        kernel,
        out_shape=tuple(outs),
        in_specs=[IN_VMEM] * len(ins),
        out_specs=(IN_VMEM,) * len(outs),
        scratch_shapes=list(scratch),
        compiler_params=pltpu.CompilerParams(vmem_limit_bytes=16 * 2**20),
        cost_estimate=pl.CostEstimate(
            flops=int(flops), bytes_accessed=int(size), transcendentals=0
        ),
        name=name,
    )(*ins)


def per_device(queries, passages, loss_grad, teacher_logits, passage_ids):
    rows, depth = queries.shape
    width = passages.shape[0]
    quarter, half = rows // 4, rows // 2
    blocks, groups = lax.axis_size("blk"), lax.axis_size("grp")
    blk_index, grp_index = lax.axis_index("blk"), lax.axis_index("grp")
    f32, bf16 = jnp.float32, jnp.bfloat16
    score_scale = 3.0 / math.sqrt(depth)

    def along(by):
        return [
            (b * groups + g, (b + by) % blocks * groups + g)
            for b in range(blocks)
            for g in range(groups)
        ]

    def across(turn):
        return [
            (b * groups + g, b * groups + (g ^ turn))
            for b in range(blocks)
            for g in range(groups)
        ]

    def move(x, pairs):
        return lax.ppermute(x, AXES, pairs)

    stat = shape((8, rows), f32)
    piece = shape((quarter, depth), bf16)
    pack = shape((24, rows), f32)
    scale = score_scale * LOG2E

    cut = quarter * 2 // 3

    def take(pieces, name):
        return pl.pallas_call(
            functools.partial(take_kernel, pieces),
            out_shape=shape((sum(piece[2] for piece in pieces), depth), bf16),
            in_specs=[pl.BlockSpec(memory_space=pl.ANY)],
            out_specs=IN_VMEM,
            scratch_shapes=[pltpu.SemaphoreType.DMA((len(pieces),))],
            name=name,
        )(queries)

    first_out = take(((0, 0, cut),), "take_first")
    first_mine = move(first_out, along(-1))
    rest_out = take(((0, cut, quarter - cut), (2, cut, quarter - cut)), "take_rest")
    rest_mine = move(rest_out, along(-1))

    coef = (score_scale * loss_grad)[None, :]
    pack_own, pack_out = call(
        functools.partial(pack_kernel, width), [pack, pack],
        [passage_ids, teacher_logits, coef], flops=1e6, name="labels",
    )
    pack_next = move(pack_out, along(-1))
    exp_own, stat_own = call(
        functools.partial(own_kernel, scale),
        [shape((width, rows), f32), stat],
        [queries, passages],
        flops=2 * rows * width * depth,
        name="own_scores",
    )
    stat_before = move(stat_own, along(-1))
    first_mine, exp_own = lax.optimization_barrier((first_mine, exp_own))
    cross_mine = move(first_mine, across(2))
    first_other = move(first_mine, across(1))
    rest_other = move(rest_mine, across(1))
    cross_other = move(cross_mine, across(1))

    exp_next, stat_next, q_next = call(
        functools.partial(next_kernel, scale),
        [shape((width, rows), f32), stat, shape((rows, depth), bf16)],
        [first_mine, first_other, cross_mine, cross_other, rest_mine, rest_other]
        + [passages, stat_before],
        flops=2 * rows * width * depth,
        name="next_scores",
    )

    cross, core, both = (move(stat_next, across(turn)) for turn in (2, 1, 3))

    def next_grads(place, merge, stats, name):
        return call(
            functools.partial(next_grad_kernel, place, merge),
            [shape((width, half), bf16), piece, piece] + ([stat] if merge else []),
            [exp_next, pack_next, passages] + stats,
            flops=2 * half * width * depth,
            name=name,
        )

    g_b, nb_mine, nb_other, whole_next = next_grads(
        1, True, [stat_next, cross, core, both], "next_grad_b"
    )
    nb_in = move(nb_other, across(1))
    whole_own = move(whole_next, along(1))
    g_a, na_mine, na_other = next_grads(0, False, [stat_next, whole_next], "next_grad_a")
    na_in = move(na_other, across(1))
    nb = (nb_mine.astype(f32) + nb_in.astype(f32)).astype(bf16)
    nb, whole_own = lax.optimization_barrier((nb, whole_own))
    nb_cross = move(nb, across(2))
    g_own, oa_mine, oa_other, ob_mine, ob_other = call(
        own_grad_kernel,
        [shape((width, rows), bf16)] + [piece] * 4,
        [exp_own, pack_own, passages, stat_own, whole_own],
        [pltpu.VMEM((rows, depth), bf16)],
        flops=2 * rows * width * depth,
        name="own_grad",
    )
    ob = (ob_mine.astype(f32) + move(ob_other, across(1)).astype(f32)).astype(bf16)
    ob_cross = move(ob, across(2))
    oa_in = move(oa_other, across(1))
    sent = (na_mine.astype(f32) + na_in.astype(f32) + nb_cross.astype(f32)).astype(bf16)
    came = move(sent, along(1))
    (passage_grad,) = call(
        functools.partial(passage_kernel, 3, half),
        [shape((width, depth), bf16)],
        [g_own, g_b, g_a, queries, q_next],
        flops=4 * rows * width * depth,
        name="passage_grad",
    )
    query_grad = (
        oa_mine.astype(f32) + oa_in.astype(f32) + ob_cross.astype(f32) + came.astype(f32)
    ).astype(bf16)
    return query_grad, passage_grad


def solution(mesh):
    in_specs = (P("blk", None), P(("blk", "grp"), None), P("blk"), P(None, "blk"), P(None, "blk"))
    out_specs = (P(("blk", "grp"), None), P(("blk", "grp"), None))
    return jax.shard_map(
        per_device, mesh=mesh, in_specs=in_specs, out_specs=out_specs, check_vma=False
    )
```

```python
import functools
import math

import jax
import jax.numpy as jnp
from jax import lax
from jax.experimental import pallas as pl
from jax.experimental.pallas import tpu as pltpu
from jax.sharding import PartitionSpec as P

AXES = ("blk", "grp")
LANE = 128
LOG2E = 1.4426950408889634
IN_VMEM = pl.BlockSpec(memory_space=pltpu.VMEM)
TILE = 256
ROWS = 64
FEW = 4


def shape(dims, dtype):
    return jax.ShapeDtypeStruct(dims, dtype)


def reorder(x, group):
    half = x.shape[1] // 2
    parts = [x[:, :half], x[:, half:]]
    parts = [jnp.where(group % 2 == 1, pltpu.roll(part, half // 2, 1), part) for part in parts]
    swap = group >= 2
    return jnp.concatenate(
        [jnp.where(swap, parts[1], parts[0]), jnp.where(swap, parts[0], parts[1])], axis=1
    )


def fill_scores(scale, p_ref, q_ref, out_ref):
    for at in range(0, q_ref.shape[0], TILE):
        to = min(at + TILE, q_ref.shape[0])
        out_ref[:, at:to] = scale * lax.dot_general(
            p_ref[...], q_ref[at:to, :], (((1,), (1,)), ((), ())),
            preferred_element_type=jnp.float32,
        )


def exponentials(ref, floor=None):
    rows, cols = ref.shape
    fold = (ROWS // 8, 8, cols)

    def find(block, top):
        at = pl.multiple_of(block * ROWS, ROWS)
        return jnp.maximum(top, jnp.max(ref[pl.ds(at, ROWS), :].reshape(fold), axis=0))

    top = lax.fori_loop(0, rows // ROWS, find, jnp.full((8, cols), -jnp.inf, jnp.float32))
    top = jnp.max(top, axis=0, keepdims=True)
    if floor is not None:
        top = jnp.maximum(top, floor)

    def raised(block, total):
        at = pl.multiple_of(block * ROWS, ROWS)
        value = jnp.exp2(ref[pl.ds(at, ROWS), :] - top)
        ref[pl.ds(at, ROWS), :] = value
        return total + jnp.sum(value.reshape(fold), axis=0)

    total = lax.fori_loop(0, rows // ROWS, raised, jnp.zeros((8, cols), jnp.float32))
    return top, jnp.sum(total, axis=0, keepdims=True)


def own_kernel(
    scale, coef_scale, q_any, p_any, ids_ref, logits_ref, loss_ref,
    exp_ref, stat_ref, pack_ref, sent_ref, q_ref, p_ref, sems,
):
    parts = sems.shape[0] - 1
    size = p_ref.shape[0] // parts
    copies = [pltpu.make_async_copy(q_any, q_ref, sems.at[parts])]
    for part in range(parts):
        rows = pl.ds(part * size, size)
        copies.append(pltpu.make_async_copy(p_any.at[rows], p_ref.at[rows], sems.at[part]))
    for copy in copies:
        copy.start()
    labels(coef_scale * loss_ref[...], ids_ref, logits_ref, pack_ref, sent_ref, p_ref.shape[0])
    copies[0].wait()
    for part in range(parts):
        copies[1 + part].wait()
        rows = pl.ds(part * size, size)
        fill_scores(scale, p_ref.at[rows], q_ref, exp_ref.at[rows])
    top, total = exponentials(exp_ref)
    for ref, at in ((stat_ref, 0), (sent_ref, 17)):
        ref[at : at + 1, :] = top
        ref[at + 1 : at + 2, :] = total


def next_kernel(scale, *refs):
    pieces, p_ref, before_ref, exp_ref, stat_ref, rows_ref = refs[:6], *refs[6:]
    first_mine, first_other, cross_mine, cross_other, rest_mine, rest_other = pieces
    cut, left = first_mine.shape[0], rest_mine.shape[0] // 2
    at = 0
    for lead, rest, skip in (
        (first_mine, rest_mine, 0),
        (first_other, rest_other, 0),
        (cross_mine, rest_mine, left),
        (cross_other, rest_other, left),
    ):
        rows_ref[at : at + cut, :] = lead[...]
        rows_ref[at + cut : at + cut + left, :] = rest[skip : skip + left, :]
        at += cut + left
    fill_scores(scale, p_ref, rows_ref, exp_ref)
    before = reorder(before_ref[16:24, :], lax.axis_index("grp"))
    top, total = exponentials(exp_ref, before[1:2])
    stat_ref[0:1, :] = top
    stat_ref[1:2, :] = total + before[2:3] * jnp.exp2(before[1:2] - top)


def labels(coef, ids_ref, logits_ref, own_ref, next_ref, width):
    device = lax.axis_index("blk") * 4 + lax.axis_index("grp")
    blocks = lax.axis_size("blk")
    before = (lax.axis_index("blk") + blocks - 1) % blocks * 4 + lax.axis_index("grp")
    ids = ids_ref[...]
    logits = logits_ref[...]
    power = jnp.exp(logits - jnp.max(logits, axis=0, keepdims=True))
    weights = coef * (power / jnp.sum(power, axis=0, keepdims=True))
    summed = jnp.zeros_like(weights)
    for k in range(8):
        summed = summed + jnp.where(ids == ids[k : k + 1], weights[k : k + 1], 0.0)
    for ref, at in ((own_ref, device), (next_ref, before)):
        place = ids - at * width
        inside = (place >= 0) & (place < width)
        places, count = [-1.0] * 8, jnp.zeros_like(coef)
        values = [0.0] * 8
        for k in range(8):
            here = inside[k : k + 1]
            for r in range(k + 1):
                chosen = here & (count == r)
                places[r] = jnp.where(chosen, place[k : k + 1].astype(jnp.float32), places[r])
                values[r] = jnp.where(chosen, summed[k : k + 1], values[r])
            count = count + here.astype(jnp.float32)
        for r in range(8):
            ref[r : r + 1, :] = places[r]
            ref[8 + r : 9 + r, :] = values[r]
        ref[16:24, :] = jnp.broadcast_to(coef, ids.shape)


def merge_stats(stat, cross, core, both):
    half = stat.shape[1] // 2
    quarter = half // 2

    def turned(x):
        return jnp.concatenate(
            [pltpu.roll(x[:, :half], quarter, 1), pltpu.roll(x[:, half:], quarter, 1)], axis=1
        )

    def crossed(x):
        return jnp.concatenate([x[:, half:], x[:, :half]], axis=1)

    parts = (stat, turned(core), crossed(cross), crossed(turned(both)))
    top = functools.reduce(jnp.maximum, [part[0:1] for part in parts])
    return top, sum(part[1:2] * jnp.exp2(part[0:1] - top) for part in parts)


def fill_grads(exp_ref, grad_ref, factor, ids, weights):
    rows, cols = exp_ref.shape
    lead = lax.broadcasted_iota(jnp.int32, (16, cols), 0)

    def fill(count):
        def step(block, carry):
            at = pl.multiple_of(block * 16, 16)
            place = (lead + block * 16).astype(jnp.float32)
            value = jnp.zeros((16, cols), jnp.float32)
            for k in range(count):
                value = jnp.where(ids[k : k + 1] == place, weights[k : k + 1], value)
            grad_ref[pl.ds(at, 16), :] = (factor * exp_ref[pl.ds(at, 16), :] - value).astype(
                jnp.bfloat16
            )
            return carry

        return step

    lax.fori_loop(0, rows // 16, fill(FEW), 0)
    more = ids[FEW:]
    low = jnp.min(jnp.where(more >= 0, more, float(rows))).astype(jnp.int32)
    high = jnp.max(more).astype(jnp.int32)
    lax.fori_loop(low // 16, jnp.where(high >= 0, high // 16 + 1, 0), fill(8), 0)


def query_product(grad_ref, p_ref, out):
    for at in range(0, p_ref.shape[1], TILE):
        out(
            at,
            lax.dot_general(
                grad_ref[...], p_ref[:, at : at + TILE], (((0,), (0,)), ((), ())),
                preferred_element_type=jnp.float32,
            ).astype(jnp.bfloat16),
        )


def next_grad_kernel(place, merge, exp_ref, pack_ref, p_ref, stat_ref, *refs):
    group = lax.axis_index("grp")
    if merge:
        cross_ref, core_ref, both_ref, grad_ref, mine_ref, other_ref, whole_ref = refs
        top, total = merge_stats(stat_ref[...], cross_ref[...], core_ref[...], both_ref[...])
        whole_ref[0:1, :] = top
        whole_ref[1:2, :] = total
    else:
        whole_ref, grad_ref, mine_ref, other_ref = refs
        top, total = whole_ref[0:1, :], whole_ref[1:2, :]
    quarter = mine_ref.shape[0]
    lanes = slice(place * 2 * quarter, (place + 1) * 2 * quarter)
    pack = reorder(pack_ref[...], group)[:, lanes]
    factor = pack[16:17] * (jnp.exp2(stat_ref[0:1, lanes] - top[:, lanes]) / total[:, lanes])
    fill_grads(exp_ref.at[:, lanes], grad_ref, factor, pack[0:8], pack[8:16])

    def put(at, part):
        mine_ref[:, at : at + TILE] = part[:quarter]
        other_ref[:, at : at + TILE] = part[quarter:]

    query_product(grad_ref, p_ref, put)


def own_grad_kernel(exp_ref, pack_ref, p_ref, stat_ref, whole_ref, grad_ref, *outs):
    *outs, rows_ref = outs
    group = lax.axis_index("grp")
    whole = reorder(whole_ref[...], group)
    factor = pack_ref[16:17, :] * (jnp.exp2(stat_ref[0:1, :] - whole[0:1]) / whole[1:2])
    fill_grads(exp_ref, grad_ref, factor, pack_ref[0:8, :], pack_ref[8:16, :])

    def put(at, part):
        rows_ref[:, at : at + TILE] = part

    query_product(grad_ref, p_ref, put)
    quarter = outs[0].shape[0]
    for slot in range(4):
        first = pl.multiple_of((group ^ slot) * quarter, quarter)
        outs[slot][...] = rows_ref[pl.ds(first, quarter), :]


def passage_kernel(count, half, *refs):
    grads, (rows_ref, next_ref, out_ref) = refs[:count], refs[count:]
    rows = (rows_ref, next_ref.at[half:, :], next_ref.at[:half, :])
    for at in range(0, out_ref.shape[1], TILE):
        out_ref[:, at : at + TILE] = sum(
            jnp.dot(
                grad_ref[...], rows_ref[:, at : at + TILE], preferred_element_type=jnp.float32
            )
            for grad_ref, rows_ref in zip(grads, rows)
        ).astype(jnp.bfloat16)


def take_kernel(pieces, q_ref, out_ref, sems):
    quarter = q_ref.shape[0] // 4
    group = lax.axis_index("grp")
    copies, at = [], 0
    for place, (slot, skip, rows) in enumerate(pieces):
        first = pl.multiple_of((group ^ slot) * quarter + skip, 16)
        copies.append(
            pltpu.make_async_copy(
                q_ref.at[pl.ds(first, rows)], out_ref.at[pl.ds(at, rows)], sems.at[place]
            )
        )
        at += rows
    for copy in copies:
        copy.start()
    for copy in copies:
        copy.wait()


def call(kernel, outs, ins, scratch=(), flops=0, name=None, anywhere=0):
    size = sum(math.prod(o.shape) * o.dtype.itemsize for o in list(outs) + list(ins))
    return pl.pallas_call(
        kernel,
        out_shape=tuple(outs),
        in_specs=[pl.BlockSpec(memory_space=pl.ANY)] * anywhere
        + [IN_VMEM] * (len(ins) - anywhere),
        out_specs=(IN_VMEM,) * len(outs),
        scratch_shapes=list(scratch),
        compiler_params=pltpu.CompilerParams(vmem_limit_bytes=24 * 2**20),
        cost_estimate=pl.CostEstimate(
            flops=int(flops), bytes_accessed=int(size), transcendentals=0
        ),
        name=name,
    )(*ins)


def per_device(queries, passages, loss_grad, teacher_logits, passage_ids):
    rows, depth = queries.shape
    width = passages.shape[0]
    quarter, half = rows // 4, rows // 2
    blocks, groups = lax.axis_size("blk"), lax.axis_size("grp")
    blk_index, grp_index = lax.axis_index("blk"), lax.axis_index("grp")
    f32, bf16 = jnp.float32, jnp.bfloat16
    score_scale = 3.0 / math.sqrt(depth)

    def along(by):
        return [
            (b * groups + g, (b + by) % blocks * groups + g)
            for b in range(blocks)
            for g in range(groups)
        ]

    def across(turn):
        return [
            (b * groups + g, b * groups + (g ^ turn))
            for b in range(blocks)
            for g in range(groups)
        ]

    def move(x, pairs):
        return lax.ppermute(x, AXES, pairs)

    stat = shape((8, rows), f32)
    piece = shape((quarter, depth), bf16)
    pack = shape((24, rows), f32)
    scale = score_scale * LOG2E

    cut = quarter * 7 // 12

    def take(pieces, name):
        return pl.pallas_call(
            functools.partial(take_kernel, pieces),
            out_shape=shape((sum(piece[2] for piece in pieces), depth), bf16),
            in_specs=[pl.BlockSpec(memory_space=pl.ANY)],
            out_specs=IN_VMEM,
            scratch_shapes=[pltpu.SemaphoreType.DMA((len(pieces),))],
            name=name,
        )(queries)

    first_out = take(((0, 0, cut),), "take_first")
    first_mine = move(first_out, along(-1))
    rest_out = take(((0, cut, quarter - cut), (2, cut, quarter - cut)), "take_rest")
    rest_mine = move(rest_out, along(-1))

    exp_own, stat_own, pack_own, pack_out = call(
        functools.partial(own_kernel, scale, score_scale),
        [shape((width, rows), f32), stat, pack, pack],
        [queries, passages, passage_ids, teacher_logits, loss_grad[None, :]],
        [
            pltpu.VMEM((rows, depth), bf16),
            pltpu.VMEM((width, depth), bf16),
            pltpu.SemaphoreType.DMA((4,)),
        ],
        flops=2 * rows * width * depth,
        name="own_scores",
        anywhere=2,
    )
    pack_next = move(pack_out, along(-1))
    first_mine, stat_own = lax.optimization_barrier((first_mine, stat_own))
    cross_mine = move(first_mine, across(2))
    first_other = move(first_mine, across(1))
    rest_mine, first_other, pack_next = lax.optimization_barrier(
        (rest_mine, first_other, pack_next)
    )
    rest_other = move(rest_mine, across(1))
    cross_other = move(cross_mine, across(1))

    exp_next, stat_next, q_next = call(
        functools.partial(next_kernel, scale),
        [shape((width, rows), f32), stat, shape((rows, depth), bf16)],
        [first_mine, first_other, cross_mine, cross_other, rest_mine, rest_other]
        + [passages, pack_next],
        flops=2 * rows * width * depth,
        name="next_scores",
    )

    cross, core, both = (move(stat_next, across(turn)) for turn in (2, 1, 3))

    def next_grads(place, merge, stats, name):
        return call(
            functools.partial(next_grad_kernel, place, merge),
            [shape((width, half), bf16), piece, piece] + ([stat] if merge else []),
            [exp_next, pack_next, passages] + stats,
            flops=2 * half * width * depth,
            name=name,
        )

    g_b, nb_mine, nb_other, whole_next = next_grads(
        1, True, [stat_next, cross, core, both], "next_grad_b"
    )
    nb_in = move(nb_other, across(1))
    whole_own = move(whole_next, along(1))
    nb = (nb_mine.astype(f32) + nb_in.astype(f32)).astype(bf16)
    nb, exp_next = lax.optimization_barrier((nb, exp_next))
    whole_own, exp_next = lax.optimization_barrier((whole_own, exp_next))
    nb_cross = move(nb, across(2))
    g_a, na_mine, na_other = next_grads(0, False, [stat_next, whole_next], "next_grad_a")
    na_in = move(na_other, across(1))
    g_own, oa_mine, oa_other, ob_mine, ob_other = call(
        own_grad_kernel,
        [shape((width, rows), bf16)] + [piece] * 4,
        [exp_own, pack_own, passages, stat_own, whole_own],
        [pltpu.VMEM((rows, depth), bf16)],
        flops=2 * rows * width * depth,
        name="own_grad",
    )
    ob = (ob_mine.astype(f32) + move(ob_other, across(1)).astype(f32)).astype(bf16)
    ob_cross = move(ob, across(2))
    oa_in = move(oa_other, across(1))
    sent = (na_mine.astype(f32) + na_in.astype(f32) + nb_cross.astype(f32)).astype(bf16)
    came = move(sent, along(1))
    (passage_grad,) = call(
        functools.partial(passage_kernel, 3, half),
        [shape((width, depth), bf16)],
        [g_own, g_b, g_a, queries, q_next],
        flops=4 * rows * width * depth,
        name="passage_grad",
    )
    query_grad = (
        oa_mine.astype(f32) + oa_in.astype(f32) + ob_cross.astype(f32) + came.astype(f32)
    ).astype(bf16)
    return query_grad, passage_grad


def solution(mesh):
    in_specs = (P("blk", None), P(("blk", "grp"), None), P("blk"), P(None, "blk"), P(None, "blk"))
    out_specs = (P(("blk", "grp"), None), P(("blk", "grp"), None))
    return jax.shard_map(
        per_device, mesh=mesh, in_specs=in_specs, out_specs=out_specs, check_vma=False
    )
```

```python
import functools
import math

import jax
import jax.numpy as jnp
from jax import lax
from jax.experimental import pallas as pl
from jax.experimental.pallas import tpu as pltpu
from jax.sharding import PartitionSpec as P

AXES = ("blk", "grp")
LANE = 128
LOG2E = 1.4426950408889634
IN_VMEM = pl.BlockSpec(memory_space=pltpu.VMEM)
TILE = 256
ROWS = 64
FEW = 4


def shape(dims, dtype):
    return jax.ShapeDtypeStruct(dims, dtype)


def reorder(x, group):
    half = x.shape[1] // 2
    parts = [x[:, :half], x[:, half:]]
    parts = [jnp.where(group % 2 == 1, pltpu.roll(part, half // 2, 1), part) for part in parts]
    swap = group >= 2
    return jnp.concatenate(
        [jnp.where(swap, parts[1], parts[0]), jnp.where(swap, parts[0], parts[1])], axis=1
    )


def fill_scores(scale, p_ref, q_ref, out_ref):
    for at in range(0, q_ref.shape[0], TILE):
        to = min(at + TILE, q_ref.shape[0])
        out_ref[:, at:to] = scale * lax.dot_general(
            p_ref[...], q_ref[at:to, :], (((1,), (1,)), ((), ())),
            preferred_element_type=jnp.float32,
        )


def exponentials(ref, floor=None):
    rows, cols = ref.shape
    fold = (ROWS // 8, 8, cols)

    def find(block, top):
        at = pl.multiple_of(block * ROWS, ROWS)
        return jnp.maximum(top, jnp.max(ref[pl.ds(at, ROWS), :].reshape(fold), axis=0))

    top = lax.fori_loop(0, rows // ROWS, find, jnp.full((8, cols), -jnp.inf, jnp.float32))
    top = jnp.max(top, axis=0, keepdims=True)
    if floor is not None:
        top = jnp.maximum(top, floor)

    def raised(block, total):
        at = pl.multiple_of(block * ROWS, ROWS)
        value = jnp.exp2(ref[pl.ds(at, ROWS), :] - top)
        ref[pl.ds(at, ROWS), :] = value
        return total + jnp.sum(value.reshape(fold), axis=0)

    total = lax.fori_loop(0, rows // ROWS, raised, jnp.zeros((8, cols), jnp.float32))
    return top, jnp.sum(total, axis=0, keepdims=True)


def own_kernel(
    scale, coef_scale, q_hbm, p_hbm, ids_ref, logits_ref, loss_ref,
    exp_ref, stat_ref, pack_ref, sent_ref, q_ref, p_ref, sems,
):
    group = lax.axis_index("grp")
    parts = sems.shape[0] - 4
    quarter, size = q_ref.shape[0] // 4, p_ref.shape[0] // parts
    copies = []
    for slot in range(4):
        first = pl.multiple_of((group ^ slot) * quarter, 16)
        copies.append(
            pltpu.make_async_copy(
                q_hbm.at[pl.ds(first, quarter)],
                q_ref.at[pl.ds(slot * quarter, quarter)],
                sems.at[slot],
            )
        )
    for part in range(parts):
        rows = pl.ds(part * size, size)
        copies.append(pltpu.make_async_copy(p_hbm.at[rows], p_ref.at[rows], sems.at[4 + part]))
    for copy in copies:
        copy.start()
    labels(coef_scale * loss_ref[...], ids_ref, logits_ref, pack_ref, sent_ref, p_ref.shape[0])
    pack_ref[...] = reorder(pack_ref[...], group)
    sent_ref[...] = reorder(sent_ref[...], group)
    for copy in copies[:4]:
        copy.wait()
    for part in range(parts):
        copies[4 + part].wait()
        rows = pl.ds(part * size, size)
        fill_scores(scale, p_ref.at[rows], q_ref, exp_ref.at[rows])
    top, total = exponentials(exp_ref)
    for ref, at in ((stat_ref, 0), (sent_ref, 17)):
        ref[at : at + 1, :] = top
        ref[at + 1 : at + 2, :] = total


def next_kernel(scale, *refs):
    pieces, p_ref, before_ref, exp_ref, stat_ref, rows_ref = refs[:6], *refs[6:]
    first_mine, first_other, cross_mine, cross_other, rest_mine, rest_other = pieces
    cut, left = first_mine.shape[0], rest_mine.shape[0] // 2
    at = 0
    for lead, rest, skip in (
        (first_mine, rest_mine, 0),
        (first_other, rest_other, 0),
        (cross_mine, rest_mine, left),
        (cross_other, rest_other, left),
    ):
        rows_ref[at : at + cut, :] = lead[...]
        rows_ref[at + cut : at + cut + left, :] = rest[skip : skip + left, :]
        at += cut + left
    fill_scores(scale, p_ref, rows_ref, exp_ref)
    before = before_ref[16:24, :]
    top, total = exponentials(exp_ref, before[1:2])
    stat_ref[0:1, :] = top
    stat_ref[1:2, :] = total + before[2:3] * jnp.exp2(before[1:2] - top)


def labels(coef, ids_ref, logits_ref, own_ref, next_ref, width):
    device = lax.axis_index("blk") * 4 + lax.axis_index("grp")
    blocks = lax.axis_size("blk")
    before = (lax.axis_index("blk") + blocks - 1) % blocks * 4 + lax.axis_index("grp")
    ids = ids_ref[...]
    logits = logits_ref[...]
    power = jnp.exp(logits - jnp.max(logits, axis=0, keepdims=True))
    weights = coef * (power / jnp.sum(power, axis=0, keepdims=True))
    summed = jnp.zeros_like(weights)
    for k in range(8):
        summed = summed + jnp.where(ids == ids[k : k + 1], weights[k : k + 1], 0.0)
    for ref, at in ((own_ref, device), (next_ref, before)):
        place = ids - at * width
        inside = (place >= 0) & (place < width)
        places, count = [-1.0] * 8, jnp.zeros_like(coef)
        values = [0.0] * 8
        for k in range(8):
            here = inside[k : k + 1]
            for r in range(k + 1):
                chosen = here & (count == r)
                places[r] = jnp.where(chosen, place[k : k + 1].astype(jnp.float32), places[r])
                values[r] = jnp.where(chosen, summed[k : k + 1], values[r])
            count = count + here.astype(jnp.float32)
        for r in range(8):
            ref[r : r + 1, :] = places[r]
            ref[8 + r : 9 + r, :] = values[r]
        ref[16:24, :] = jnp.broadcast_to(coef, ids.shape)


def merge_stats(stat, cross, core, both):
    half = stat.shape[1] // 2
    quarter = half // 2

    def turned(x):
        return jnp.concatenate(
            [pltpu.roll(x[:, :half], quarter, 1), pltpu.roll(x[:, half:], quarter, 1)], axis=1
        )

    def crossed(x):
        return jnp.concatenate([x[:, half:], x[:, :half]], axis=1)

    parts = (stat, turned(core), crossed(cross), crossed(turned(both)))
    top = functools.reduce(jnp.maximum, [part[0:1] for part in parts])
    return top, sum(part[1:2] * jnp.exp2(part[0:1] - top) for part in parts)


def fill_grads(exp_ref, grad_ref, factor, ids, weights):
    rows, cols = exp_ref.shape
    lead = lax.broadcasted_iota(jnp.int32, (16, cols), 0)

    def fill(count):
        def step(block, carry):
            at = pl.multiple_of(block * 16, 16)
            place = (lead + block * 16).astype(jnp.float32)
            value = jnp.zeros((16, cols), jnp.float32)
            for k in range(count):
                value = jnp.where(ids[k : k + 1] == place, weights[k : k + 1], value)
            grad_ref[pl.ds(at, 16), :] = (factor * exp_ref[pl.ds(at, 16), :] - value).astype(
                jnp.bfloat16
            )
            return carry

        return step

    lax.fori_loop(0, rows // 16, fill(FEW), 0)
    more = ids[FEW:]
    low = jnp.min(jnp.where(more >= 0, more, float(rows))).astype(jnp.int32)
    high = jnp.max(more).astype(jnp.int32)
    lax.fori_loop(low // 16, jnp.where(high >= 0, high // 16 + 1, 0), fill(8), 0)


def query_product(grad_ref, p_ref, out):
    for at in range(0, p_ref.shape[1], TILE):
        out(
            at,
            lax.dot_general(
                grad_ref[...], p_ref[:, at : at + TILE], (((0,), (0,)), ((), ())),
                preferred_element_type=jnp.float32,
            ).astype(jnp.bfloat16),
        )


def grads_of(place, exp_ref, pack_ref, p_ref, stat_ref, whole_ref, grad_ref, mine_ref, other_ref):
    quarter = mine_ref.shape[0]
    lanes = slice(place * 2 * quarter, (place + 1) * 2 * quarter)
    factor = pack_ref[16:17, lanes] * (
        jnp.exp2(stat_ref[0:1, lanes] - whole_ref[0:1, lanes]) / whole_ref[1:2, lanes]
    )
    fill_grads(
        exp_ref.at[:, lanes], grad_ref, factor, pack_ref[0:8, lanes], pack_ref[8:16, lanes]
    )

    def put(at, part):
        mine_ref[:, at : at + TILE] = part[:quarter]
        other_ref[:, at : at + TILE] = part[quarter:]

    query_product(grad_ref, p_ref, put)


def first_grad_kernel(p_ref, exp_ref, pack_ref, stat_ref, cross_ref, core_ref, both_ref, *outs):
    *outs, whole_ref = outs
    top, total = merge_stats(stat_ref[...], cross_ref[...], core_ref[...], both_ref[...])
    whole_ref[0:1, :] = top
    whole_ref[1:2, :] = total
    grads_of(1, exp_ref, pack_ref, p_ref, stat_ref, whole_ref, *outs)


def grad_kernel(places, p_ref, *refs):
    ins, outs = refs[: 4 * len(places)], refs[4 * len(places) :]
    for n, place in enumerate(places):
        exp_ref, pack_ref, stat_ref, whole_ref = ins[4 * n : 4 * n + 4]
        grads_of(
            place, exp_ref, pack_ref, p_ref, stat_ref, whole_ref, *outs[3 * n : 3 * n + 3]
        )


def passage_kernel(half, *refs):
    grads, (own_ref, next_ref, out_ref) = refs[:4], refs[4:]
    rows = [ref.at[at : at + half, :] for ref in (own_ref, next_ref) for at in (0, half)]
    for at in range(0, out_ref.shape[1], TILE):
        out_ref[:, at : at + TILE] = sum(
            jnp.dot(
                grad_ref[...], rows_ref[:, at : at + TILE], preferred_element_type=jnp.float32
            )
            for grad_ref, rows_ref in zip(grads, rows)
        ).astype(jnp.bfloat16)


def take_kernel(pieces, q_ref, out_ref, sems):
    quarter = q_ref.shape[0] // 4
    group = lax.axis_index("grp")
    copies, at = [], 0
    for place, (slot, skip, rows) in enumerate(pieces):
        first = pl.multiple_of((group ^ slot) * quarter + skip, 16)
        copies.append(
            pltpu.make_async_copy(
                q_ref.at[pl.ds(first, rows)], out_ref.at[pl.ds(at, rows)], sems.at[place]
            )
        )
        at += rows
    for copy in copies:
        copy.start()
    for copy in copies:
        copy.wait()


def call(kernel, outs, ins, scratch=(), flops=0, name=None, anywhere=0):
    size = sum(math.prod(o.shape) * o.dtype.itemsize for o in list(outs) + list(ins))
    return pl.pallas_call(
        kernel,
        out_shape=tuple(outs),
        in_specs=[pl.BlockSpec(memory_space=pltpu.HBM)] * anywhere
        + [IN_VMEM] * (len(ins) - anywhere),
        out_specs=(IN_VMEM,) * len(outs),
        scratch_shapes=list(scratch),
        compiler_params=pltpu.CompilerParams(vmem_limit_bytes=24 * 2**20),
        cost_estimate=pl.CostEstimate(
            flops=int(flops), bytes_accessed=int(size), transcendentals=0
        ),
        name=name,
    )(*ins)


def per_device(queries, passages, loss_grad, teacher_logits, passage_ids):
    rows, depth = queries.shape
    width = passages.shape[0]
    quarter, half = rows // 4, rows // 2
    blocks, groups = lax.axis_size("blk"), lax.axis_size("grp")
    blk_index, grp_index = lax.axis_index("blk"), lax.axis_index("grp")
    f32, bf16 = jnp.float32, jnp.bfloat16
    score_scale = 3.0 / math.sqrt(depth)

    def along(by):
        return [
            (b * groups + g, (b + by) % blocks * groups + g)
            for b in range(blocks)
            for g in range(groups)
        ]

    def across(turn):
        return [
            (b * groups + g, b * groups + (g ^ turn))
            for b in range(blocks)
            for g in range(groups)
        ]

    def move(x, pairs):
        return lax.ppermute(x, AXES, pairs)

    stat = shape((8, rows), f32)
    piece = shape((quarter, depth), bf16)
    pack = shape((24, rows), f32)
    scale = score_scale * LOG2E

    cut = quarter * 7 // 12

    def take(pieces, name):
        return pl.pallas_call(
            functools.partial(take_kernel, pieces),
            out_shape=shape((sum(piece[2] for piece in pieces), depth), bf16),
            in_specs=[pl.BlockSpec(memory_space=pl.ANY)],
            out_specs=IN_VMEM,
            scratch_shapes=[pltpu.SemaphoreType.DMA((len(pieces),))],
            name=name,
        )(queries)

    first_out = take(((0, 0, cut),), "take_first")
    first_mine = move(first_out, along(-1))
    rest_out = take(((0, cut, quarter - cut), (2, cut, quarter - cut)), "take_rest")
    rest_mine = move(rest_out, along(-1))

    first_mine, loss_grad = lax.optimization_barrier((first_mine, loss_grad))
    exp_own, stat_own, pack_own, pack_out, q_own = call(
        functools.partial(own_kernel, scale, score_scale),
        [shape((width, rows), f32), stat, pack, pack, shape((rows, depth), bf16)],
        [queries, passages, passage_ids, teacher_logits, loss_grad[None, :]],
        [
            pltpu.VMEM((width, depth), bf16),
            pltpu.SemaphoreType.DMA((7,)),
        ],
        flops=2 * rows * width * depth,
        name="own_scores",
        anywhere=2,
    )
    pack_next = move(pack_out, along(-1))
    cross_mine = move(first_mine, across(2))
    first_other = move(first_mine, across(1))
    rest_mine, first_other, pack_next = lax.optimization_barrier(
        (rest_mine, first_other, pack_next)
    )
    rest_other = move(rest_mine, across(1))
    cross_other = move(cross_mine, across(1))

    exp_next, stat_next, q_next = call(
        functools.partial(next_kernel, scale),
        [shape((width, rows), f32), stat, shape((rows, depth), bf16)],
        [first_mine, first_other, cross_mine, cross_other, rest_mine, rest_other]
        + [passages, pack_next],
        flops=2 * rows * width * depth,
        name="next_scores",
    )

    cross, core, both = (move(stat_next, across(turn)) for turn in (2, 1, 3))

    def grads(kernel, ins, count, more, name):
        return call(
            kernel,
            [shape((width, half), bf16), piece, piece] * count + more,
            [passages] + ins,
            flops=2 * count * half * width * depth,
            name=name,
        )

    g_b, nb_mine, nb_other, whole_next = grads(
        first_grad_kernel, [exp_next, pack_next, stat_next, cross, core, both], 1, [stat],
        "next_grad_b",
    )
    nb_in = move(nb_other, across(1))
    whole_own = move(whole_next, along(1))
    nb = (nb_mine.astype(f32) + nb_in.astype(f32)).astype(bf16)
    nb, exp_next = lax.optimization_barrier((nb, exp_next))
    nb_cross = move(nb, across(2))
    of_next = [exp_next, pack_next, stat_next, whole_next]
    of_own = [exp_own, pack_own, stat_own, whole_own]
    g_a, na_mine, na_other, g_ob, ob_mine, ob_other = grads(
        functools.partial(grad_kernel, (0, 1)), of_next + of_own, 2, [], "next_a_own_b"
    )
    na_in = move(na_other, across(1))
    ob_in = move(ob_other, across(1))
    ob_mine, nb_cross = lax.optimization_barrier((ob_mine, nb_cross))
    ob = (ob_mine.astype(f32) + ob_in.astype(f32)).astype(bf16)
    ob_cross = move(ob, across(2))
    g_oa, oa_mine, oa_other = grads(
        functools.partial(grad_kernel, (0,)), of_own, 1, [], "own_grad_a"
    )
    oa_in = move(oa_other, across(1))
    sent = (na_mine.astype(f32) + na_in.astype(f32) + nb_cross.astype(f32)).astype(bf16)
    came = move(sent, along(1))
    (passage_grad,) = call(
        functools.partial(passage_kernel, half),
        [shape((width, depth), bf16)],
        [g_oa, g_ob, g_a, g_b, q_own, q_next],
        flops=4 * rows * width * depth,
        name="passage_grad",
    )
    query_grad = (
        oa_mine.astype(f32) + oa_in.astype(f32) + ob_cross.astype(f32) + came.astype(f32)
    ).astype(bf16)
    return query_grad, passage_grad


def solution(mesh):
    in_specs = (P("blk", None), P(("blk", "grp"), None), P("blk"), P(None, "blk"), P(None, "blk"))
    out_specs = (P(("blk", "grp"), None), P(("blk", "grp"), None))
    return jax.shard_map(
        per_device, mesh=mesh, in_specs=in_specs, out_specs=out_specs, check_vma=False
    )
```

```python
import functools
import math

import jax
import jax.numpy as jnp
from jax import lax
from jax.experimental import pallas as pl
from jax.experimental.pallas import tpu as pltpu
from jax.sharding import PartitionSpec as P

AXES = ("blk", "grp")
LANE = 128
LOG2E = 1.4426950408889634
IN_VMEM = pl.BlockSpec(memory_space=pltpu.VMEM)
TILE = 256
PARTS = 6
STEPS = 3
FEW = 4


def shape(dims, dtype):
    return jax.ShapeDtypeStruct(dims, dtype)


def reorder(x, group):
    half = x.shape[1] // 2
    parts = [x[:, :half], x[:, half:]]
    parts = [jnp.where(group % 2 == 1, pltpu.roll(part, half // 2, 1), part) for part in parts]
    swap = group >= 2
    return jnp.concatenate(
        [jnp.where(swap, parts[1], parts[0]), jnp.where(swap, parts[0], parts[1])], axis=1
    )


def scores(scale, p_ref, q_ref, exp_ref, stat_ref, before=None):
    size = p_ref.shape[0] // PARTS
    tops, totals = [], []
    for part in range(PARTS):
        rows = slice(part * size, (part + 1) * size)
        values = scale * lax.dot_general(
            p_ref[rows, :], q_ref[...], (((1,), (1,)), ((), ())),
            preferred_element_type=jnp.float32,
        )
        fold = (size // 8, 8, values.shape[1])
        top = jnp.max(jnp.max(values.reshape(fold), axis=0), axis=0, keepdims=True)
        values = jnp.exp2(values - top)
        exp_ref[rows, :] = values
        total = jnp.sum(jnp.sum(values.reshape(fold), axis=0), axis=0, keepdims=True)
        stat_ref[2 + part : 3 + part, :] = top
        tops.append(top)
        totals.append(total)
    if before is not None:
        tops.append(before[0:1])
        totals.append(before[1:2])
    whole = functools.reduce(jnp.maximum, tops)
    stat_ref[0:1, :] = whole
    stat_ref[1:2, :] = sum(total * jnp.exp2(top - whole) for top, total in zip(tops, totals))


def own_kernel(
    scale, coef_scale, q_hbm, p_ref, ids_ref, logits_ref, loss_ref,
    exp_ref, stat_ref, pack_ref, sent_ref, q_ref, sems,
):
    group = lax.axis_index("grp")
    quarter = q_ref.shape[0] // 4
    copies = []
    for slot in range(4):
        first = pl.multiple_of((group ^ slot) * quarter, 16)
        copies.append(
            pltpu.make_async_copy(
                q_hbm.at[pl.ds(first, quarter)],
                q_ref.at[pl.ds(slot * quarter, quarter)],
                sems.at[slot],
            )
        )
    for copy in copies:
        copy.start()
    labels(coef_scale * loss_ref[...], ids_ref, logits_ref, pack_ref, sent_ref, p_ref.shape[0])
    pack_ref[...] = reorder(pack_ref[...], group)
    sent_ref[...] = reorder(sent_ref[...], group)
    for copy in copies:
        copy.wait()
    scores(scale, p_ref, q_ref, exp_ref, stat_ref)


def next_kernel(scale, *refs):
    pieces, p_ref, before_ref, exp_ref, stat_ref, rows_ref = refs[:6], *refs[6:]
    first_mine, first_other, cross_mine, cross_other, rest_mine, rest_other = pieces
    cut, left = first_mine.shape[0], rest_mine.shape[0] // 2
    at = 0
    for lead, rest, skip in (
        (first_mine, rest_mine, 0),
        (first_other, rest_other, 0),
        (cross_mine, rest_mine, left),
        (cross_other, rest_other, left),
    ):
        rows_ref[at : at + cut, :] = lead[...]
        rows_ref[at + cut : at + cut + left, :] = rest[skip : skip + left, :]
        at += cut + left
    scores(scale, p_ref, rows_ref, exp_ref, stat_ref, before_ref[...])


def labels(coef, ids_ref, logits_ref, own_ref, next_ref, width):
    device = lax.axis_index("blk") * 4 + lax.axis_index("grp")
    blocks = lax.axis_size("blk")
    before = (lax.axis_index("blk") + blocks - 1) % blocks * 4 + lax.axis_index("grp")
    ids = ids_ref[...]
    logits = logits_ref[...]
    power = jnp.exp(logits - jnp.max(logits, axis=0, keepdims=True))
    weights = coef * (power / jnp.sum(power, axis=0, keepdims=True))
    summed = jnp.zeros_like(weights)
    for k in range(8):
        summed = summed + jnp.where(ids == ids[k : k + 1], weights[k : k + 1], 0.0)
    for ref, at in ((own_ref, device), (next_ref, before)):
        place = ids - at * width
        inside = (place >= 0) & (place < width)
        places, count = [-1.0] * 8, jnp.zeros_like(coef)
        values = [0.0] * 8
        for k in range(8):
            here = inside[k : k + 1]
            for r in range(k + 1):
                chosen = here & (count == r)
                places[r] = jnp.where(chosen, place[k : k + 1].astype(jnp.float32), places[r])
                values[r] = jnp.where(chosen, summed[k : k + 1], values[r])
            count = count + here.astype(jnp.float32)
        for r in range(8):
            ref[r : r + 1, :] = places[r]
            ref[8 + r : 9 + r, :] = values[r]
        ref[16:24, :] = jnp.broadcast_to(coef, ids.shape)


def merge_stats(stat, cross, core, both):
    half = stat.shape[1] // 2
    quarter = half // 2

    def turned(x):
        return jnp.concatenate(
            [pltpu.roll(x[:, :half], quarter, 1), pltpu.roll(x[:, half:], quarter, 1)], axis=1
        )

    def crossed(x):
        return jnp.concatenate([x[:, half:], x[:, :half]], axis=1)

    parts = (stat, turned(core), crossed(cross), crossed(turned(both)))
    top = functools.reduce(jnp.maximum, [part[0:1] for part in parts])
    return top, sum(part[1:2] * jnp.exp2(part[0:1] - top) for part in parts)


def fill_grads(block, count, exp_ref, grad_ref, factor, ids, weights):
    cols = exp_ref.shape[1]
    rows = pl.ds(block * 16, 16)
    place = lax.broadcasted_iota(jnp.int32, (16, cols), 0) + block * 16
    place = place.astype(jnp.float32)
    value = jnp.zeros((16, cols), jnp.float32)
    for k in range(count):
        value = jnp.where(ids[k : k + 1] == place, weights[k : k + 1], value)
    grad_ref[rows, :] = (factor * exp_ref[rows, :] - value).astype(jnp.bfloat16)


def grads_of(
    place, exp_ref, pack_ref, p_ref, stat_ref, whole_ref, grad_ref, mine_ref, other_ref,
    total_ref,
):
    quarter = mine_ref.shape[0]
    lanes = slice(place * 2 * quarter, (place + 1) * 2 * quarter)
    whole = whole_ref[0:2, lanes]
    coef = pack_ref[16:17, lanes] / whole[1:2]
    factors = coef * jnp.exp2(stat_ref[2 : 2 + PARTS, lanes] - whole[0:1])
    ids, weights = pack_ref[0:8, lanes], pack_ref[8:16, lanes]
    exps = exp_ref.at[:, lanes]
    rows = exp_ref.shape[0]
    more = ids[FEW:]
    low = jnp.min(jnp.where(more >= 0, more, float(rows))).astype(jnp.int32) // 16
    high = jnp.max(more).astype(jnp.int32)
    high = jnp.where(high >= 0, high // 16 + 1, 0)
    size = rows // STEPS
    for step in range(STEPS):
        first, last = step * size // 16, (step + 1) * size // 16
        for block in range(first, last):
            part = block * 16 * PARTS // rows
            fill_grads(
                block, FEW, exps, grad_ref, factors[part : part + 1], ids, weights
            )

        def again(block, carry):
            part = block // (rows // PARTS // 16)
            factor = factors[0:1]
            for n in range(1, PARTS):
                factor = jnp.where(part == n, factors[n : n + 1], factor)
            fill_grads(block, 8, exps, grad_ref, factor, ids, weights)
            return carry

        lax.fori_loop(jnp.maximum(low, first), jnp.minimum(high, last), again, 0)
        taken = slice(step * size, (step + 1) * size)
        for at in range(0, p_ref.shape[1], TILE):
            cols = slice(at, at + TILE)
            part = lax.dot_general(
                grad_ref[taken, :], p_ref[taken, cols], (((0,), (0,)), ((), ())),
                preferred_element_type=jnp.float32,
            )
            if step > 0:
                part = total_ref[:, cols] + part
            if step < STEPS - 1:
                total_ref[:, cols] = part
            else:
                mine_ref[:, cols] = part[:quarter].astype(jnp.bfloat16)
                other_ref[:, cols] = part[quarter:].astype(jnp.bfloat16)


def first_grad_kernel(p_ref, exp_ref, pack_ref, stat_ref, cross_ref, core_ref, both_ref, *outs):
    *outs, whole_ref, total_ref = outs
    top, total = merge_stats(stat_ref[...], cross_ref[...], core_ref[...], both_ref[...])
    whole_ref[0:1, :] = top
    whole_ref[1:2, :] = total
    grads_of(1, exp_ref, pack_ref, p_ref, stat_ref, whole_ref, *outs, total_ref)


def grad_kernel(places, p_ref, *refs):
    ins, outs, total_ref = refs[: 4 * len(places)], refs[4 * len(places) : -1], refs[-1]
    for n, place in enumerate(places):
        exp_ref, pack_ref, stat_ref, whole_ref = ins[4 * n : 4 * n + 4]
        grads_of(
            place, exp_ref, pack_ref, p_ref, stat_ref, whole_ref, *outs[3 * n : 3 * n + 3],
            total_ref,
        )


def passage_kernel(half, *refs):
    grads, (own_ref, next_ref, out_ref) = refs[:4], refs[4:]
    rows = [ref.at[at : at + half, :] for ref in (own_ref, next_ref) for at in (0, half)]
    for at in range(0, out_ref.shape[1], TILE):
        out_ref[:, at : at + TILE] = sum(
            jnp.dot(
                grad_ref[...], rows_ref[:, at : at + TILE], preferred_element_type=jnp.float32
            )
            for grad_ref, rows_ref in zip(grads, rows)
        ).astype(jnp.bfloat16)


def take_kernel(pieces, q_ref, out_ref, sems):
    quarter = q_ref.shape[0] // 4
    group = lax.axis_index("grp")
    copies, at = [], 0
    for place, (slot, skip, rows) in enumerate(pieces):
        first = pl.multiple_of((group ^ slot) * quarter + skip, 16)
        copies.append(
            pltpu.make_async_copy(
                q_ref.at[pl.ds(first, rows)], out_ref.at[pl.ds(at, rows)], sems.at[place]
            )
        )
        at += rows
    for copy in copies:
        copy.start()
    for copy in copies:
        copy.wait()


def call(kernel, outs, ins, scratch=(), flops=0, name=None, anywhere=0):
    size = sum(math.prod(o.shape) * o.dtype.itemsize for o in list(outs) + list(ins))
    return pl.pallas_call(
        kernel,
        out_shape=tuple(outs),
        in_specs=[pl.BlockSpec(memory_space=pltpu.HBM)] * anywhere
        + [IN_VMEM] * (len(ins) - anywhere),
        out_specs=(IN_VMEM,) * len(outs),
        scratch_shapes=list(scratch),
        compiler_params=pltpu.CompilerParams(vmem_limit_bytes=24 * 2**20),
        cost_estimate=pl.CostEstimate(
            flops=int(flops), bytes_accessed=int(size), transcendentals=0
        ),
        name=name,
    )(*ins)


def per_device(queries, passages, loss_grad, teacher_logits, passage_ids):
    rows, depth = queries.shape
    width = passages.shape[0]
    quarter, half = rows // 4, rows // 2
    blocks, groups = lax.axis_size("blk"), lax.axis_size("grp")
    blk_index, grp_index = lax.axis_index("blk"), lax.axis_index("grp")
    f32, bf16 = jnp.float32, jnp.bfloat16
    score_scale = 3.0 / math.sqrt(depth)

    def along(by):
        return [
            (b * groups + g, (b + by) % blocks * groups + g)
            for b in range(blocks)
            for g in range(groups)
        ]

    def across(turn):
        return [
            (b * groups + g, b * groups + (g ^ turn))
            for b in range(blocks)
            for g in range(groups)
        ]

    def move(x, pairs):
        return lax.ppermute(x, AXES, pairs)

    stat = shape((8, rows), f32)
    piece = shape((quarter, depth), bf16)
    pack = shape((24, rows), f32)
    scale = score_scale * LOG2E

    cut = quarter * 7 // 12

    def take(pieces, name):
        return pl.pallas_call(
            functools.partial(take_kernel, pieces),
            out_shape=shape((sum(piece[2] for piece in pieces), depth), bf16),
            in_specs=[pl.BlockSpec(memory_space=pl.ANY)],
            out_specs=IN_VMEM,
            scratch_shapes=[pltpu.SemaphoreType.DMA((len(pieces),))],
            name=name,
        )(queries)

    first_out = take(((0, 0, cut),), "take_first")
    first_mine = move(first_out, along(-1))
    rest_out = take(((0, cut, quarter - cut), (2, cut, quarter - cut)), "take_rest")
    rest_mine = move(rest_out, along(-1))

    exp_own, stat_own, pack_own, pack_out, q_own = call(
        functools.partial(own_kernel, scale, score_scale),
        [shape((width, rows), f32), stat, pack, pack, shape((rows, depth), bf16)],
        [pltpu.with_memory_space_constraint(queries, pltpu.HBM), passages, passage_ids, teacher_logits, loss_grad[None, :]],
        [
            pltpu.SemaphoreType.DMA((4,)),
        ],
        flops=2 * rows * width * depth,
        name="own_scores",
        anywhere=1,
    )
    stat_before = move(stat_own, along(-1))
    first_mine, stat_own = lax.optimization_barrier((first_mine, stat_own))
    cross_mine = move(first_mine, across(2))
    first_other = move(first_mine, across(1))
    rest_mine, first_other, stat_before = lax.optimization_barrier(
        (rest_mine, first_other, stat_before)
    )
    rest_other = move(rest_mine, across(1))
    rest_mine, pack_out = lax.optimization_barrier((rest_mine, pack_out))
    pack_next = move(pack_out, along(-1))
    cross_other = move(cross_mine, across(1))

    exp_next, stat_next, q_next = call(
        functools.partial(next_kernel, scale),
        [shape((width, rows), f32), stat, shape((rows, depth), bf16)],
        [first_mine, first_other, cross_mine, cross_other, rest_mine, rest_other]
        + [passages, stat_before],
        flops=2 * rows * width * depth,
        name="next_scores",
    )

    cross, core, both = (move(stat_next, across(turn)) for turn in (2, 1, 3))

    def grads(kernel, ins, count, more, name):
        return call(
            kernel,
            [shape((width, half), bf16), piece, piece] * count + more,
            [passages] + ins,
            [pltpu.VMEM((half, depth), f32)],
            flops=2 * count * half * width * depth,
            name=name,
        )

    g_b, nb_mine, nb_other, whole_next = grads(
        first_grad_kernel, [exp_next, pack_next, stat_next, cross, core, both], 1, [stat],
        "next_grad_b",
    )
    nb_in = move(nb_other, across(1))
    whole_own = move(whole_next, along(1))
    nb = (nb_mine.astype(f32) + nb_in.astype(f32)).astype(bf16)
    nb, exp_next = lax.optimization_barrier((nb, exp_next))
    whole_own, exp_next = lax.optimization_barrier((whole_own, exp_next))
    nb_cross = move(nb, across(2))
    g_a, na_mine, na_other = grads(
        functools.partial(grad_kernel, (0,)), [exp_next, pack_next, stat_next, whole_next], 1, [],
        "next_grad_a",
    )
    na_in = move(na_other, across(1))
    of_own = [exp_own, pack_own, stat_own, whole_own]
    g_ob, ob_mine, ob_other, g_oa, oa_mine, oa_other = grads(
        functools.partial(grad_kernel, (1, 0)), of_own + of_own, 2, [], "own_grad"
    )
    ob_in = move(ob_other, across(1))
    oa_in = move(oa_other, across(1))
    ob_mine, nb_cross = lax.optimization_barrier((ob_mine, nb_cross))
    ob = (ob_mine.astype(f32) + ob_in.astype(f32)).astype(bf16)
    came_across = move(ob, across(2))
    sent = (na_mine.astype(f32) + na_in.astype(f32) + nb_cross.astype(f32)).astype(bf16)
    came_along = move(sent, along(1))
    (passage_grad,) = call(
        functools.partial(passage_kernel, half),
        [shape((width, depth), bf16)],
        [g_oa, g_ob, g_a, g_b, q_own, q_next],
        flops=4 * rows * width * depth,
        name="passage_grad",
    )
    query_grad = (
        oa_mine.astype(f32)
        + oa_in.astype(f32)
        + came_along.astype(f32)
        + came_across.astype(f32)
    ).astype(bf16)
    return query_grad, passage_grad


def solution(mesh):
    in_specs = (P("blk", None), P(("blk", "grp"), None), P("blk"), P(None, "blk"), P(None, "blk"))
    out_specs = (P(("blk", "grp"), None), P(("blk", "grp"), None))
    return jax.shard_map(
        per_device, mesh=mesh, in_specs=in_specs, out_specs=out_specs, check_vma=False
    )
```

```python
import functools
import math

import jax
import jax.numpy as jnp
from jax import lax
from jax.experimental import pallas as pl
from jax.experimental.pallas import tpu as pltpu
from jax.sharding import PartitionSpec as P

AXES = ("blk", "grp")
LANE = 128
LOG2E = 1.4426950408889634
IN_VMEM = pl.BlockSpec(memory_space=pltpu.VMEM)
TILE = 256
PARTS = 6
STEPS = 3
FEW = 4


def shape(dims, dtype):
    return jax.ShapeDtypeStruct(dims, dtype)


def reorder(x, group):
    half = x.shape[1] // 2
    parts = [x[:, :half], x[:, half:]]
    parts = [jnp.where(group % 2 == 1, pltpu.roll(part, half // 2, 1), part) for part in parts]
    swap = group >= 2
    return jnp.concatenate(
        [jnp.where(swap, parts[1], parts[0]), jnp.where(swap, parts[0], parts[1])], axis=1
    )


def scores(scale, p_ref, q_ref, exp_ref, stat_ref):
    size = p_ref.shape[0] // PARTS
    tops, totals = [], []
    for part in range(PARTS):
        rows = slice(part * size, (part + 1) * size)
        values = scale * lax.dot_general(
            p_ref[rows, :], q_ref[...], (((1,), (1,)), ((), ())),
            preferred_element_type=jnp.float32,
        )
        fold = (size // 8, 8, values.shape[1])
        top = jnp.max(jnp.max(values.reshape(fold), axis=0), axis=0, keepdims=True)
        values = jnp.exp2(values - top)
        exp_ref[rows, :] = values
        total = jnp.sum(jnp.sum(values.reshape(fold), axis=0), axis=0, keepdims=True)
        stat_ref[2 + part : 3 + part, :] = top
        tops.append(top)
        totals.append(total)
    whole = functools.reduce(jnp.maximum, tops)
    stat_ref[0:1, :] = whole
    stat_ref[1:2, :] = sum(total * jnp.exp2(top - whole) for top, total in zip(tops, totals))


def own_kernel(
    scale, coef_scale, q_hbm, p_ref, ids_ref, logits_ref, loss_ref,
    exp_ref, stat_ref, pack_ref, sent_ref, q_ref, sems,
):
    group = lax.axis_index("grp")
    quarter = q_ref.shape[0] // 4
    copies = []
    for slot in range(4):
        first = pl.multiple_of((group ^ slot) * quarter, 16)
        copies.append(
            pltpu.make_async_copy(
                q_hbm.at[pl.ds(first, quarter)],
                q_ref.at[pl.ds(slot * quarter, quarter)],
                sems.at[slot],
            )
        )
    for copy in copies:
        copy.start()
    labels(coef_scale * loss_ref[...], ids_ref, logits_ref, pack_ref, sent_ref, p_ref.shape[0])
    pack_ref[...] = reorder(pack_ref[...], group)
    sent_ref[...] = reorder(sent_ref[...], group)
    for copy in copies:
        copy.wait()
    scores(scale, p_ref, q_ref, exp_ref, stat_ref)


def next_kernel(scale, place, mine_ref, other_ref, p_ref, *refs):
    exp_ref, stat_ref, rows_ref = refs[-3:]
    quarter = mine_ref.shape[0]
    half = 2 * quarter
    rows_ref[:quarter, :] = mine_ref[...]
    rows_ref[quarter:, :] = other_ref[...]
    if place == 1:
        known_ref, before_ref = refs[:2]
        stat_ref[:, :half] = known_ref[:, :half]
    scores(scale, p_ref, rows_ref, exp_ref, stat_ref.at[:, place * half : (place + 1) * half])
    if place == 1:
        top = jnp.maximum(stat_ref[0:1, :], before_ref[0:1, :])
        stat_ref[1:2, :] = stat_ref[1:2, :] * jnp.exp2(stat_ref[0:1, :] - top) + before_ref[
            1:2, :
        ] * jnp.exp2(before_ref[0:1, :] - top)
        stat_ref[0:1, :] = top


def labels(coef, ids_ref, logits_ref, own_ref, next_ref, width):
    device = lax.axis_index("blk") * 4 + lax.axis_index("grp")
    blocks = lax.axis_size("blk")
    before = (lax.axis_index("blk") + blocks - 1) % blocks * 4 + lax.axis_index("grp")
    ids = ids_ref[...]
    logits = logits_ref[...]
    power = jnp.exp(logits - jnp.max(logits, axis=0, keepdims=True))
    weights = coef * (power / jnp.sum(power, axis=0, keepdims=True))
    summed = jnp.zeros_like(weights)
    for k in range(8):
        summed = summed + jnp.where(ids == ids[k : k + 1], weights[k : k + 1], 0.0)
    for ref, at in ((own_ref, device), (next_ref, before)):
        place = ids - at * width
        inside = (place >= 0) & (place < width)
        places, count = [-1.0] * 8, jnp.zeros_like(coef)
        values = [0.0] * 8
        for k in range(8):
            here = inside[k : k + 1]
            for r in range(k + 1):
                chosen = here & (count == r)
                places[r] = jnp.where(chosen, place[k : k + 1].astype(jnp.float32), places[r])
                values[r] = jnp.where(chosen, summed[k : k + 1], values[r])
            count = count + here.astype(jnp.float32)
        for r in range(8):
            ref[r : r + 1, :] = places[r]
            ref[8 + r : 9 + r, :] = values[r]
        ref[16:24, :] = jnp.broadcast_to(coef, ids.shape)


def merge_stats(stat, cross, core, both):
    half = stat.shape[1] // 2
    quarter = half // 2

    def turned(x):
        return jnp.concatenate(
            [pltpu.roll(x[:, :half], quarter, 1), pltpu.roll(x[:, half:], quarter, 1)], axis=1
        )

    def crossed(x):
        return jnp.concatenate([x[:, half:], x[:, :half]], axis=1)

    parts = (stat, turned(core), crossed(cross), crossed(turned(both)))
    top = functools.reduce(jnp.maximum, [part[0:1] for part in parts])
    return top, sum(part[1:2] * jnp.exp2(part[0:1] - top) for part in parts)


def fill_grads(block, count, exp_ref, grad_ref, factor, ids, weights):
    cols = exp_ref.shape[1]
    rows = pl.ds(block * 16, 16)
    place = lax.broadcasted_iota(jnp.int32, (16, cols), 0) + block * 16
    place = place.astype(jnp.float32)
    value = jnp.zeros((16, cols), jnp.float32)
    for k in range(count):
        value = jnp.where(ids[k : k + 1] == place, weights[k : k + 1], value)
    grad_ref[rows, :] = (factor * exp_ref[rows, :] - value).astype(jnp.bfloat16)


def grads_of(
    place, exp_ref, pack_ref, p_ref, stat_ref, whole_ref, grad_ref, mine_ref, other_ref,
    total_ref,
):
    quarter = mine_ref.shape[0]
    lanes = slice(place * 2 * quarter, (place + 1) * 2 * quarter)
    whole = whole_ref[0:2, lanes]
    coef = pack_ref[16:17, lanes] / whole[1:2]
    factors = coef * jnp.exp2(stat_ref[2 : 2 + PARTS, lanes] - whole[0:1])
    ids, weights = pack_ref[0:8, lanes], pack_ref[8:16, lanes]
    exps = exp_ref if exp_ref.shape[1] == 2 * quarter else exp_ref.at[:, lanes]
    rows = exp_ref.shape[0]
    more = ids[FEW:]
    low = jnp.min(jnp.where(more >= 0, more, float(rows))).astype(jnp.int32) // 16
    high = jnp.max(more).astype(jnp.int32)
    high = jnp.where(high >= 0, high // 16 + 1, 0)
    size = rows // STEPS
    for step in range(STEPS):
        first, last = step * size // 16, (step + 1) * size // 16
        for block in range(first, last):
            part = block * 16 * PARTS // rows
            fill_grads(
                block, FEW, exps, grad_ref, factors[part : part + 1], ids, weights
            )

        def again(block, carry):
            part = block // (rows // PARTS // 16)
            factor = factors[0:1]
            for n in range(1, PARTS):
                factor = jnp.where(part == n, factors[n : n + 1], factor)
            fill_grads(block, 8, exps, grad_ref, factor, ids, weights)
            return carry

        lax.fori_loop(jnp.maximum(low, first), jnp.minimum(high, last), again, 0)
        taken = slice(step * size, (step + 1) * size)
        for at in range(0, p_ref.shape[1], TILE):
            cols = slice(at, at + TILE)
            part = lax.dot_general(
                grad_ref[taken, :], p_ref[taken, cols], (((0,), (0,)), ((), ())),
                preferred_element_type=jnp.float32,
            )
            if step > 0:
                part = total_ref[:, cols] + part
            if step < STEPS - 1:
                total_ref[:, cols] = part
            else:
                mine_ref[:, cols] = part[:quarter].astype(jnp.bfloat16)
                other_ref[:, cols] = part[quarter:].astype(jnp.bfloat16)


def first_grad_kernel(p_ref, exp_ref, pack_ref, stat_ref, cross_ref, core_ref, both_ref, *outs):
    *outs, whole_ref, total_ref = outs
    top, total = merge_stats(stat_ref[...], cross_ref[...], core_ref[...], both_ref[...])
    whole_ref[0:1, :] = top
    whole_ref[1:2, :] = total
    grads_of(1, exp_ref, pack_ref, p_ref, stat_ref, whole_ref, *outs, total_ref)


def grad_kernel(places, p_ref, *refs):
    ins, outs, total_ref = refs[: 4 * len(places)], refs[4 * len(places) : -1], refs[-1]
    for n, place in enumerate(places):
        exp_ref, pack_ref, stat_ref, whole_ref = ins[4 * n : 4 * n + 4]
        grads_of(
            place, exp_ref, pack_ref, p_ref, stat_ref, whole_ref, *outs[3 * n : 3 * n + 3],
            total_ref,
        )


def passage_kernel(half, *refs):
    grads, (own_ref, *rows, out_ref) = refs[:4], refs[4:]
    rows = [own_ref.at[at : at + half, :] for at in (0, half)] + rows
    for at in range(0, out_ref.shape[1], TILE):
        out_ref[:, at : at + TILE] = sum(
            jnp.dot(
                grad_ref[...], rows_ref[:, at : at + TILE], preferred_element_type=jnp.float32
            )
            for grad_ref, rows_ref in zip(grads, rows)
        ).astype(jnp.bfloat16)


def take_kernel(slot, q_ref, out_ref, sem):
    quarter = out_ref.shape[0]
    first = pl.multiple_of((lax.axis_index("grp") ^ slot) * quarter, 16)
    copy = pltpu.make_async_copy(q_ref.at[pl.ds(first, quarter)], out_ref, sem)
    copy.start()
    copy.wait()


def call(kernel, outs, ins, scratch=(), flops=0, name=None, anywhere=0):
    size = sum(math.prod(o.shape) * o.dtype.itemsize for o in list(outs) + list(ins))
    return pl.pallas_call(
        kernel,
        out_shape=tuple(outs),
        in_specs=[pl.BlockSpec(memory_space=pltpu.HBM)] * anywhere
        + [IN_VMEM] * (len(ins) - anywhere),
        out_specs=(IN_VMEM,) * len(outs),
        scratch_shapes=list(scratch),
        compiler_params=pltpu.CompilerParams(vmem_limit_bytes=24 * 2**20),
        cost_estimate=pl.CostEstimate(
            flops=int(flops), bytes_accessed=int(size), transcendentals=0
        ),
        name=name,
    )(*ins)


def per_device(queries, passages, loss_grad, teacher_logits, passage_ids):
    rows, depth = queries.shape
    width = passages.shape[0]
    quarter, half = rows // 4, rows // 2
    blocks, groups = lax.axis_size("blk"), lax.axis_size("grp")
    blk_index, grp_index = lax.axis_index("blk"), lax.axis_index("grp")
    f32, bf16 = jnp.float32, jnp.bfloat16
    score_scale = 3.0 / math.sqrt(depth)

    def along(by):
        return [
            (b * groups + g, (b + by) % blocks * groups + g)
            for b in range(blocks)
            for g in range(groups)
        ]

    def across(turn):
        return [
            (b * groups + g, b * groups + (g ^ turn))
            for b in range(blocks)
            for g in range(groups)
        ]

    def move(x, pairs):
        return lax.ppermute(x, AXES, pairs)

    stat = shape((8, rows), f32)
    piece = shape((quarter, depth), bf16)
    pack = shape((24, rows), f32)
    scale = score_scale * LOG2E

    def take(slot, name):
        return pl.pallas_call(
            functools.partial(take_kernel, slot),
            out_shape=piece,
            in_specs=[pl.BlockSpec(memory_space=pl.ANY)],
            out_specs=IN_VMEM,
            scratch_shapes=[pltpu.SemaphoreType.DMA(())],
            name=name,
        )(queries)

    a_mine = move(take(0, "take_a"), along(-1))
    b_mine = move(take(2, "take_b"), along(-1))

    exp_own, stat_own, pack_own, pack_out, q_own = call(
        functools.partial(own_kernel, scale, score_scale),
        [shape((width, rows), f32), stat, pack, pack, shape((rows, depth), bf16)],
        [pltpu.with_memory_space_constraint(queries, pltpu.HBM), passages, passage_ids, teacher_logits, loss_grad[None, :]],
        [
            pltpu.SemaphoreType.DMA((4,)),
        ],
        flops=2 * rows * width * depth,
        name="own_scores",
        anywhere=1,
    )
    stat_before = move(stat_own, along(-1))
    a_mine, stat_own = lax.optimization_barrier((a_mine, stat_own))
    a_other = move(a_mine, across(1))

    def next_scores(place, ins, name):
        return call(
            functools.partial(next_kernel, scale, place),
            [shape((width, half), f32), stat, shape((half, depth), bf16)],
            ins,
            flops=2 * half * width * depth,
            name=name,
        )

    exp_a, stat_a, q_a = next_scores(0, [a_mine, a_other, passages], "next_scores_a")
    b_mine, stat_before = lax.optimization_barrier((b_mine, stat_before))
    b_other = move(b_mine, across(1))
    b_mine, pack_out = lax.optimization_barrier((b_mine, pack_out))
    pack_next = move(pack_out, along(-1))
    exp_b, stat_next, q_b = next_scores(
        1, [b_mine, b_other, passages, stat_a, stat_before], "next_scores_b"
    )

    cross, core, both = (move(stat_next, across(turn)) for turn in (2, 1, 3))

    def grads(kernel, ins, count, more, name):
        return call(
            kernel,
            [shape((width, half), bf16), piece, piece] * count + more,
            [passages] + ins,
            [pltpu.VMEM((half, depth), f32)],
            flops=2 * count * half * width * depth,
            name=name,
        )

    g_b, nb_mine, nb_other, whole_next = grads(
        first_grad_kernel, [exp_b, pack_next, stat_next, cross, core, both], 1, [stat],
        "next_grad_b",
    )
    nb_in = move(nb_other, across(1))
    whole_own = move(whole_next, along(1))
    nb = (nb_mine.astype(f32) + nb_in.astype(f32)).astype(bf16)
    nb, exp_a = lax.optimization_barrier((nb, exp_a))
    nb_cross = move(nb, across(2))
    g_a, na_mine, na_other = grads(
        functools.partial(grad_kernel, (0,)), [exp_a, pack_next, stat_next, whole_next], 1, [],
        "next_grad_a",
    )
    na_in = move(na_other, across(1))
    of_own = [exp_own, pack_own, stat_own, whole_own]
    g_ob, ob_mine, ob_other, g_oa, oa_mine, oa_other = grads(
        functools.partial(grad_kernel, (1, 0)), of_own + of_own, 2, [], "own_grad"
    )
    ob_in = move(ob_other, across(1))
    oa_in = move(oa_other, across(1))
    ob_mine, nb_cross = lax.optimization_barrier((ob_mine, nb_cross))
    ob = (ob_mine.astype(f32) + ob_in.astype(f32)).astype(bf16)
    came_across = move(ob, across(2))
    sent = (na_mine.astype(f32) + na_in.astype(f32) + nb_cross.astype(f32)).astype(bf16)
    came_along = move(sent, along(1))
    (passage_grad,) = call(
        functools.partial(passage_kernel, half),
        [shape((width, depth), bf16)],
        [g_oa, g_ob, g_a, g_b, q_own, q_a, q_b],
        flops=4 * rows * width * depth,
        name="passage_grad",
    )
    query_grad = (
        oa_mine.astype(f32)
        + oa_in.astype(f32)
        + came_along.astype(f32)
        + came_across.astype(f32)
    ).astype(bf16)
    return query_grad, passage_grad


def solution(mesh):
    in_specs = (P("blk", None), P(("blk", "grp"), None), P("blk"), P(None, "blk"), P(None, "blk"))
    out_specs = (P(("blk", "grp"), None), P(("blk", "grp"), None))
    return jax.shard_map(
        per_device, mesh=mesh, in_specs=in_specs, out_specs=out_specs, check_vma=False
    )
```

```python
import functools
import math

import jax
import jax.numpy as jnp
from jax import lax
from jax.experimental import pallas as pl
from jax.experimental.pallas import tpu as pltpu
from jax.sharding import PartitionSpec as P

AXES = ("blk", "grp")
LANE = 128
LOG2E = 1.4426950408889634
IN_VMEM = pl.BlockSpec(memory_space=pltpu.VMEM)
TILE = 256
PARTS = 6
STEPS = 3
FEW = 4


def shape(dims, dtype):
    return jax.ShapeDtypeStruct(dims, dtype)


def reorder(x, group):
    half = x.shape[1] // 2
    parts = [x[:, :half], x[:, half:]]
    parts = [jnp.where(group % 2 == 1, pltpu.roll(part, half // 2, 1), part) for part in parts]
    swap = group >= 2
    return jnp.concatenate(
        [jnp.where(swap, parts[1], parts[0]), jnp.where(swap, parts[0], parts[1])], axis=1
    )


def scores(scale, p_ref, q_ref, exp_ref, stat_ref):
    size = p_ref.shape[0] // PARTS
    tops, totals = [], []
    for part in range(PARTS):
        rows = slice(part * size, (part + 1) * size)
        values = scale * lax.dot_general(
            p_ref[rows, :], q_ref[...], (((1,), (1,)), ((), ())),
            preferred_element_type=jnp.float32,
        )
        fold = (size // 8, 8, values.shape[1])
        top = jnp.max(jnp.max(values.reshape(fold), axis=0), axis=0, keepdims=True)
        values = jnp.exp2(values - top)
        exp_ref[rows, :] = values
        total = jnp.sum(jnp.sum(values.reshape(fold), axis=0), axis=0, keepdims=True)
        stat_ref[2 + part : 3 + part, :] = top
        tops.append(top)
        totals.append(total)
    whole = functools.reduce(jnp.maximum, tops)
    stat_ref[0:1, :] = whole
    stat_ref[1:2, :] = sum(total * jnp.exp2(top - whole) for top, total in zip(tops, totals))


def own_kernel(
    scale, coef_scale, q_hbm, p_ref, ids_ref, logits_ref, loss_ref,
    exp_ref, stat_ref, pack_ref, sent_ref, q_ref, sems,
):
    group = lax.axis_index("grp")
    quarter = q_ref.shape[0] // 4
    copies = []
    for slot in range(4):
        first = pl.multiple_of((group ^ slot) * quarter, 16)
        copies.append(
            pltpu.make_async_copy(
                q_hbm.at[pl.ds(first, quarter)],
                q_ref.at[pl.ds(slot * quarter, quarter)],
                sems.at[slot],
            )
        )
    for copy in copies:
        copy.start()
    labels(coef_scale * loss_ref[...], ids_ref, logits_ref, pack_ref, sent_ref, p_ref.shape[0])
    pack_ref[...] = reorder(pack_ref[...], group)
    sent_ref[...] = reorder(sent_ref[...], group)
    for copy in copies:
        copy.wait()
    scores(scale, p_ref, q_ref, exp_ref, stat_ref)


def next_kernel(scale, place, mine_ref, other_ref, p_ref, *refs):
    exp_ref, stat_ref, rows_ref = refs[-3:]
    quarter = mine_ref.shape[0]
    half = 2 * quarter
    rows_ref[:quarter, :] = mine_ref[...]
    rows_ref[quarter:, :] = other_ref[...]
    if place == 1:
        known_ref, before_ref = refs[:2]
        stat_ref[:, :half] = known_ref[:, :half]
    scores(scale, p_ref, rows_ref, exp_ref, stat_ref.at[:, place * half : (place + 1) * half])
    if place == 1:
        top = jnp.maximum(stat_ref[0:1, :], before_ref[0:1, :])
        stat_ref[1:2, :] = stat_ref[1:2, :] * jnp.exp2(stat_ref[0:1, :] - top) + before_ref[
            1:2, :
        ] * jnp.exp2(before_ref[0:1, :] - top)
        stat_ref[0:1, :] = top


def labels(coef, ids_ref, logits_ref, own_ref, next_ref, width):
    device = lax.axis_index("blk") * 4 + lax.axis_index("grp")
    blocks = lax.axis_size("blk")
    before = (lax.axis_index("blk") + blocks - 1) % blocks * 4 + lax.axis_index("grp")
    ids = ids_ref[...]
    logits = logits_ref[...]
    power = jnp.exp(logits - jnp.max(logits, axis=0, keepdims=True))
    weights = coef * (power / jnp.sum(power, axis=0, keepdims=True))
    summed = jnp.zeros_like(weights)
    for k in range(8):
        summed = summed + jnp.where(ids == ids[k : k + 1], weights[k : k + 1], 0.0)
    for ref, at in ((own_ref, device), (next_ref, before)):
        place = ids - at * width
        inside = (place >= 0) & (place < width)
        places, count = [-1.0] * 8, jnp.zeros_like(coef)
        values = [0.0] * 8
        for k in range(8):
            here = inside[k : k + 1]
            for r in range(k + 1):
                chosen = here & (count == r)
                places[r] = jnp.where(chosen, place[k : k + 1].astype(jnp.float32), places[r])
                values[r] = jnp.where(chosen, summed[k : k + 1], values[r])
            count = count + here.astype(jnp.float32)
        for r in range(8):
            ref[r : r + 1, :] = places[r]
            ref[8 + r : 9 + r, :] = values[r]
        ref[16:24, :] = jnp.broadcast_to(coef, ids.shape)


def merge_stats(stat, cross, core, both):
    half = stat.shape[1] // 2
    quarter = half // 2

    def turned(x):
        return jnp.concatenate(
            [pltpu.roll(x[:, :half], quarter, 1), pltpu.roll(x[:, half:], quarter, 1)], axis=1
        )

    def crossed(x):
        return jnp.concatenate([x[:, half:], x[:, :half]], axis=1)

    parts = (stat, turned(core), crossed(cross), crossed(turned(both)))
    top = functools.reduce(jnp.maximum, [part[0:1] for part in parts])
    return top, sum(part[1:2] * jnp.exp2(part[0:1] - top) for part in parts)


def fill_grads(block, count, exp_ref, grad_ref, factor, ids, weights):
    cols = exp_ref.shape[1]
    rows = pl.ds(block * 16, 16)
    place = lax.broadcasted_iota(jnp.int32, (16, cols), 0) + block * 16
    place = place.astype(jnp.float32)
    value = jnp.zeros((16, cols), jnp.float32)
    for k in range(count):
        value = jnp.where(ids[k : k + 1] == place, weights[k : k + 1], value)
    grad_ref[rows, :] = (factor * exp_ref[rows, :] - value).astype(jnp.bfloat16)


def grads_of(
    place, exp_ref, pack_ref, p_ref, stat_ref, whole_ref, grad_ref, mine_ref, other_ref,
    total_ref,
):
    quarter = mine_ref.shape[0]
    lanes = slice(place * 2 * quarter, (place + 1) * 2 * quarter)
    whole = whole_ref[0:2, lanes]
    coef = pack_ref[16:17, lanes] / whole[1:2]
    factors = coef * jnp.exp2(stat_ref[2 : 2 + PARTS, lanes] - whole[0:1])
    ids, weights = pack_ref[0:8, lanes], pack_ref[8:16, lanes]
    exps = exp_ref if exp_ref.shape[1] == 2 * quarter else exp_ref.at[:, lanes]
    rows = exp_ref.shape[0]
    more = ids[FEW:]
    low = jnp.min(jnp.where(more >= 0, more, float(rows))).astype(jnp.int32) // 16
    high = jnp.max(more).astype(jnp.int32)
    high = jnp.where(high >= 0, high // 16 + 1, 0)
    size = rows // STEPS
    for step in range(STEPS):
        first, last = step * size // 16, (step + 1) * size // 16
        for block in range(first, last):
            part = block * 16 * PARTS // rows
            fill_grads(
                block, FEW, exps, grad_ref, factors[part : part + 1], ids, weights
            )

        def again(block, carry):
            part = block // (rows // PARTS // 16)
            factor = factors[0:1]
            for n in range(1, PARTS):
                factor = jnp.where(part == n, factors[n : n + 1], factor)
            fill_grads(block, 8, exps, grad_ref, factor, ids, weights)
            return carry

        lax.fori_loop(jnp.maximum(low, first), jnp.minimum(high, last), again, 0)
        taken = slice(step * size, (step + 1) * size)
        for at in range(0, p_ref.shape[1], TILE):
            cols = slice(at, at + TILE)
            part = lax.dot_general(
                grad_ref[taken, :], p_ref[taken, cols], (((0,), (0,)), ((), ())),
                preferred_element_type=jnp.float32,
            )
            if step > 0:
                part = total_ref[:, cols] + part
            if step < STEPS - 1:
                total_ref[:, cols] = part
            else:
                mine_ref[:, cols] = part[:quarter].astype(jnp.bfloat16)
                other_ref[:, cols] = part[quarter:].astype(jnp.bfloat16)


def first_grad_kernel(p_ref, exp_ref, pack_ref, stat_ref, cross_ref, core_ref, both_ref, *outs):
    *outs, whole_ref, total_ref = outs
    top, total = merge_stats(stat_ref[...], cross_ref[...], core_ref[...], both_ref[...])
    whole_ref[0:1, :] = top
    whole_ref[1:2, :] = total
    grads_of(1, exp_ref, pack_ref, p_ref, stat_ref, whole_ref, *outs, total_ref)


def grad_kernel(places, p_ref, *refs):
    ins, outs, total_ref = refs[: 4 * len(places)], refs[4 * len(places) : -1], refs[-1]
    for n, place in enumerate(places):
        exp_ref, pack_ref, stat_ref, whole_ref = ins[4 * n : 4 * n + 4]
        grads_of(
            place, exp_ref, pack_ref, p_ref, stat_ref, whole_ref, *outs[3 * n : 3 * n + 3],
            total_ref,
        )


def passage_kernel(half, *refs):
    grads, (own_ref, *rows, out_ref) = refs[:4], refs[4:]
    rows = [own_ref.at[at : at + half, :] for at in (0, half)] + rows
    for at in range(0, out_ref.shape[1], TILE):
        out_ref[:, at : at + TILE] = sum(
            jnp.dot(
                grad_ref[...], rows_ref[:, at : at + TILE], preferred_element_type=jnp.float32
            )
            for grad_ref, rows_ref in zip(grads, rows)
        ).astype(jnp.bfloat16)


def take_kernel(slot, q_ref, out_ref, sem):
    quarter = out_ref.shape[0]
    first = pl.multiple_of((lax.axis_index("grp") ^ slot) * quarter, 16)
    copy = pltpu.make_async_copy(q_ref.at[pl.ds(first, quarter)], out_ref, sem)
    copy.start()
    copy.wait()


def call(kernel, outs, ins, scratch=(), flops=0, name=None, anywhere=0):
    size = sum(math.prod(o.shape) * o.dtype.itemsize for o in list(outs) + list(ins))
    return pl.pallas_call(
        kernel,
        out_shape=tuple(outs),
        in_specs=[pl.BlockSpec(memory_space=pltpu.HBM)] * anywhere
        + [IN_VMEM] * (len(ins) - anywhere),
        out_specs=(IN_VMEM,) * len(outs),
        scratch_shapes=list(scratch),
        compiler_params=pltpu.CompilerParams(vmem_limit_bytes=24 * 2**20),
        cost_estimate=pl.CostEstimate(
            flops=int(flops), bytes_accessed=int(size), transcendentals=0
        ),
        name=name,
    )(*ins)


def per_device(queries, passages, loss_grad, teacher_logits, passage_ids):
    rows, depth = queries.shape
    width = passages.shape[0]
    quarter, half = rows // 4, rows // 2
    blocks, groups = lax.axis_size("blk"), lax.axis_size("grp")
    blk_index, grp_index = lax.axis_index("blk"), lax.axis_index("grp")
    f32, bf16 = jnp.float32, jnp.bfloat16
    score_scale = 3.0 / math.sqrt(depth)

    def along(by):
        return [
            (b * groups + g, (b + by) % blocks * groups + g)
            for b in range(blocks)
            for g in range(groups)
        ]

    def across(turn):
        return [
            (b * groups + g, b * groups + (g ^ turn))
            for b in range(blocks)
            for g in range(groups)
        ]

    def move(x, pairs):
        return lax.ppermute(x, AXES, pairs)

    stat = shape((8, rows), f32)
    piece = shape((quarter, depth), bf16)
    pack = shape((24, rows), f32)
    scale = score_scale * LOG2E

    def take(slot, name):
        return pl.pallas_call(
            functools.partial(take_kernel, slot),
            out_shape=piece,
            in_specs=[pl.BlockSpec(memory_space=pl.ANY)],
            out_specs=IN_VMEM,
            scratch_shapes=[pltpu.SemaphoreType.DMA(())],
            name=name,
        )(queries)

    a_mine = move(take(0, "take_a"), along(-1))
    b_mine = move(take(2, "take_b"), along(-1))

    exp_own, stat_own, pack_own, pack_out, q_own = call(
        functools.partial(own_kernel, scale, score_scale),
        [shape((width, rows), f32), stat, pack, pack, shape((rows, depth), bf16)],
        [pltpu.with_memory_space_constraint(queries, pltpu.HBM), passages, passage_ids, teacher_logits, loss_grad[None, :]],
        [
            pltpu.SemaphoreType.DMA((4,)),
        ],
        flops=2 * rows * width * depth,
        name="own_scores",
        anywhere=1,
    )
    stat_before = move(stat_own, along(-1))
    a_mine, stat_own = lax.optimization_barrier((a_mine, stat_own))
    a_other = move(a_mine, across(1))

    def next_scores(place, ins, name):
        return call(
            functools.partial(next_kernel, scale, place),
            [shape((width, half), f32), stat, shape((half, depth), bf16)],
            ins,
            flops=2 * half * width * depth,
            name=name,
        )

    exp_a, stat_a, q_a = next_scores(0, [a_mine, a_other, passages], "next_scores_a")
    b_mine, stat_before = lax.optimization_barrier((b_mine, stat_before))
    b_other = move(b_mine, across(1))
    b_mine, pack_out = lax.optimization_barrier((b_mine, pack_out))
    pack_next = move(pack_out, along(-1))
    exp_b, stat_next, q_b = next_scores(
        1, [b_mine, b_other, passages, stat_a, stat_before], "next_scores_b"
    )

    cross, core, both = (move(stat_next, across(turn)) for turn in (2, 1, 3))

    def grads(kernel, ins, count, more, name):
        return call(
            kernel,
            [shape((width, half), bf16), piece, piece] * count + more,
            [passages] + ins,
            [pltpu.VMEM((half, depth), f32)],
            flops=2 * count * half * width * depth,
            name=name,
        )

    g_b, nb_mine, nb_other, whole_next = grads(
        first_grad_kernel, [exp_b, pack_next, stat_next, cross, core, both], 1, [stat],
        "next_grad_b",
    )
    nb_in = move(nb_other, across(1))
    nb = (nb_mine.astype(f32) + nb_in.astype(f32)).astype(bf16)
    nb, exp_a, whole_next = lax.optimization_barrier((nb, exp_a, whole_next))
    whole_own = move(whole_next, along(1))
    nb_cross = move(nb, across(2))
    g_a, na_mine, na_other = grads(
        functools.partial(grad_kernel, (0,)), [exp_a, pack_next, stat_next, whole_next], 1, [],
        "next_grad_a",
    )
    of_own = [exp_own, pack_own, stat_own, whole_own]
    g_ob, ob_mine, ob_other, g_oa, oa_mine, oa_other = grads(
        functools.partial(grad_kernel, (1, 0)), of_own + of_own, 2, [], "own_grad"
    )
    na_other, ob_other = lax.optimization_barrier((na_other, ob_other))
    na_in = move(na_other, across(1))
    ob_in = move(ob_other, across(1))
    oa_in = move(oa_other, across(1))
    ob_mine, nb_cross = lax.optimization_barrier((ob_mine, nb_cross))
    ob = (ob_mine.astype(f32) + ob_in.astype(f32)).astype(bf16)
    came_across = move(ob, across(2))
    sent = (na_mine.astype(f32) + na_in.astype(f32) + nb_cross.astype(f32)).astype(bf16)
    came_along = move(sent, along(1))
    (passage_grad,) = call(
        functools.partial(passage_kernel, half),
        [shape((width, depth), bf16)],
        [g_oa, g_ob, g_a, g_b, q_own, q_a, q_b],
        flops=4 * rows * width * depth,
        name="passage_grad",
    )
    query_grad = (
        oa_mine.astype(f32)
        + oa_in.astype(f32)
        + came_along.astype(f32)
        + came_across.astype(f32)
    ).astype(bf16)
    return query_grad, passage_grad


def solution(mesh):
    in_specs = (P("blk", None), P(("blk", "grp"), None), P("blk"), P(None, "blk"), P(None, "blk"))
    out_specs = (P(("blk", "grp"), None), P(("blk", "grp"), None))
    return jax.shard_map(
        per_device, mesh=mesh, in_specs=in_specs, out_specs=out_specs, check_vma=False
    )
```

```python
import functools
import math

import jax
import jax.numpy as jnp
from jax import lax
from jax.experimental import pallas as pl
from jax.experimental.pallas import tpu as pltpu
from jax.sharding import PartitionSpec as P

AXES = ("blk", "grp")
LANE = 128
LOG2E = 1.4426950408889634
IN_VMEM = pl.BlockSpec(memory_space=pltpu.VMEM)
TILE = 256
PARTS = 6
STEPS = 3
FEW = 4


def shape(dims, dtype):
    return jax.ShapeDtypeStruct(dims, dtype)


def reorder(x, group):
    half = x.shape[1] // 2
    parts = [x[:, :half], x[:, half:]]
    parts = [jnp.where(group % 2 == 1, pltpu.roll(part, half // 2, 1), part) for part in parts]
    swap = group >= 2
    return jnp.concatenate(
        [jnp.where(swap, parts[1], parts[0]), jnp.where(swap, parts[0], parts[1])], axis=1
    )


def scores(scale, p_ref, q_ref, exp_ref, stat_ref):
    size = p_ref.shape[0] // PARTS
    tops, totals = [], []
    for part in range(PARTS):
        rows = slice(part * size, (part + 1) * size)
        values = scale * lax.dot_general(
            p_ref[rows, :], q_ref[...], (((1,), (1,)), ((), ())),
            preferred_element_type=jnp.float32,
        )
        fold = (size // 8, 8, values.shape[1])
        top = jnp.max(jnp.max(values.reshape(fold), axis=0), axis=0, keepdims=True)
        values = jnp.exp2(values - top)
        exp_ref[rows, :] = values
        total = jnp.sum(jnp.sum(values.reshape(fold), axis=0), axis=0, keepdims=True)
        stat_ref[2 + part : 3 + part, :] = top
        tops.append(top)
        totals.append(total)
    whole = functools.reduce(jnp.maximum, tops)
    stat_ref[0:1, :] = whole
    stat_ref[1:2, :] = sum(total * jnp.exp2(top - whole) for top, total in zip(tops, totals))


def own_kernel(
    scale, coef_scale, q_hbm, p_ref, ids_ref, logits_ref, loss_ref,
    exp_ref, stat_ref, pack_ref, sent_ref, q_ref, sems,
):
    group = lax.axis_index("grp")
    quarter = q_ref.shape[0] // 4
    copies = []
    for slot in range(4):
        first = pl.multiple_of((group ^ slot) * quarter, 16)
        copies.append(
            pltpu.make_async_copy(
                q_hbm.at[pl.ds(first, quarter)],
                q_ref.at[pl.ds(slot * quarter, quarter)],
                sems.at[slot],
            )
        )
    for copy in copies:
        copy.start()
    labels(coef_scale * loss_ref[...], ids_ref, logits_ref, pack_ref, sent_ref, p_ref.shape[0])
    pack_ref[...] = reorder(pack_ref[...], group)
    sent_ref[...] = reorder(sent_ref[...], group)
    for copy in copies:
        copy.wait()
    scores(scale, p_ref, q_ref, exp_ref, stat_ref)


def next_kernel(scale, place, mine_ref, other_ref, p_ref, *refs):
    exp_ref, stat_ref, rows_ref = refs[-3:]
    quarter = mine_ref.shape[0]
    half = 2 * quarter
    rows_ref[:quarter, :] = mine_ref[...]
    rows_ref[quarter:, :] = other_ref[...]
    if place == 1:
        known_ref, before_ref = refs[:2]
        stat_ref[:, :half] = known_ref[:, :half]
    scores(scale, p_ref, rows_ref, exp_ref, stat_ref.at[:, place * half : (place + 1) * half])
    if place == 1:
        top = jnp.maximum(stat_ref[0:1, :], before_ref[0:1, :])
        stat_ref[1:2, :] = stat_ref[1:2, :] * jnp.exp2(stat_ref[0:1, :] - top) + before_ref[
            1:2, :
        ] * jnp.exp2(before_ref[0:1, :] - top)
        stat_ref[0:1, :] = top


def labels(coef, ids_ref, logits_ref, own_ref, next_ref, width):
    device = lax.axis_index("blk") * 4 + lax.axis_index("grp")
    blocks = lax.axis_size("blk")
    before = (lax.axis_index("blk") + blocks - 1) % blocks * 4 + lax.axis_index("grp")
    ids = ids_ref[...]
    logits = logits_ref[...]
    power = jnp.exp(logits - jnp.max(logits, axis=0, keepdims=True))
    weights = coef * (power / jnp.sum(power, axis=0, keepdims=True))
    summed = jnp.zeros_like(weights)
    for k in range(8):
        summed = summed + jnp.where(ids == ids[k : k + 1], weights[k : k + 1], 0.0)
    for ref, at in ((own_ref, device), (next_ref, before)):
        place = ids - at * width
        inside = (place >= 0) & (place < width)
        places, count = [-1.0] * 8, jnp.zeros_like(coef)
        values = [0.0] * 8
        for k in range(8):
            here = inside[k : k + 1]
            for r in range(k + 1):
                chosen = here & (count == r)
                places[r] = jnp.where(chosen, place[k : k + 1].astype(jnp.float32), places[r])
                values[r] = jnp.where(chosen, summed[k : k + 1], values[r])
            count = count + here.astype(jnp.float32)
        for r in range(8):
            ref[r : r + 1, :] = places[r]
            ref[8 + r : 9 + r, :] = values[r]
        ref[16:24, :] = jnp.broadcast_to(coef, ids.shape)


def merge_stats(stat, cross, core, both):
    half = stat.shape[1] // 2
    quarter = half // 2

    def turned(x):
        return jnp.concatenate(
            [pltpu.roll(x[:, :half], quarter, 1), pltpu.roll(x[:, half:], quarter, 1)], axis=1
        )

    def crossed(x):
        return jnp.concatenate([x[:, half:], x[:, :half]], axis=1)

    parts = (stat, turned(core), crossed(cross), crossed(turned(both)))
    top = functools.reduce(jnp.maximum, [part[0:1] for part in parts])
    return top, sum(part[1:2] * jnp.exp2(part[0:1] - top) for part in parts)


def fill_grads(block, count, exp_ref, grad_ref, factor, ids, weights):
    cols = exp_ref.shape[1]
    rows = pl.ds(block * 16, 16)
    place = lax.broadcasted_iota(jnp.int32, (16, cols), 0) + block * 16
    place = place.astype(jnp.float32)
    value = jnp.zeros((16, cols), jnp.float32)
    for k in range(count):
        value = jnp.where(ids[k : k + 1] == place, weights[k : k + 1], value)
    grad_ref[rows, :] = (factor * exp_ref[rows, :] - value).astype(jnp.bfloat16)


def grads_of(
    place, exp_ref, pack_ref, p_ref, stat_ref, whole_ref, grad_ref, mine_ref, other_ref,
    total_ref,
):
    quarter = mine_ref.shape[0]
    lanes = slice(place * 2 * quarter, (place + 1) * 2 * quarter)
    whole = whole_ref[0:2, lanes]
    coef = pack_ref[16:17, lanes] / whole[1:2]
    factors = coef * jnp.exp2(stat_ref[2 : 2 + PARTS, lanes] - whole[0:1])
    ids, weights = pack_ref[0:8, lanes], pack_ref[8:16, lanes]
    exps = exp_ref if exp_ref.shape[1] == 2 * quarter else exp_ref.at[:, lanes]
    grad_ref = grad_ref.at[:, lanes]
    rows = exp_ref.shape[0]
    more = ids[FEW:]
    low = jnp.min(jnp.where(more >= 0, more, float(rows))).astype(jnp.int32) // 16
    high = jnp.max(more).astype(jnp.int32)
    high = jnp.where(high >= 0, high // 16 + 1, 0)
    size = rows // STEPS
    for step in range(STEPS):
        first, last = step * size // 16, (step + 1) * size // 16
        for block in range(first, last):
            part = block * 16 * PARTS // rows
            fill_grads(
                block, FEW, exps, grad_ref, factors[part : part + 1], ids, weights
            )

        def again(block, carry):
            part = block // (rows // PARTS // 16)
            factor = factors[0:1]
            for n in range(1, PARTS):
                factor = jnp.where(part == n, factors[n : n + 1], factor)
            fill_grads(block, 8, exps, grad_ref, factor, ids, weights)
            return carry

        lax.fori_loop(jnp.maximum(low, first), jnp.minimum(high, last), again, 0)
        taken = slice(step * size, (step + 1) * size)
        for at in range(0, p_ref.shape[1], TILE):
            cols = slice(at, at + TILE)
            part = lax.dot_general(
                grad_ref[taken, :], p_ref[taken, cols], (((0,), (0,)), ((), ())),
                preferred_element_type=jnp.float32,
            )
            if step > 0:
                part = total_ref[:, cols] + part
            if step < STEPS - 1:
                total_ref[:, cols] = part
            else:
                mine_ref[:, cols] = part[:quarter].astype(jnp.bfloat16)
                other_ref[:, cols] = part[quarter:].astype(jnp.bfloat16)


def first_grad_kernel(p_ref, exp_ref, pack_ref, stat_ref, cross_ref, core_ref, both_ref, *outs):
    *outs, whole_ref, total_ref = outs
    top, total = merge_stats(stat_ref[...], cross_ref[...], core_ref[...], both_ref[...])
    whole_ref[0:1, :] = top
    whole_ref[1:2, :] = total
    grads_of(1, exp_ref, pack_ref, p_ref, stat_ref, whole_ref, *outs, total_ref)


def grad_kernel(places, p_ref, *refs):
    exp_ref, pack_ref, stat_ref, whole_ref = refs[:4]
    grad_ref, *outs, total_ref = refs[-2 - 2 * len(places) :]
    for n, place in enumerate(places):
        grads_of(
            place, exp_ref, pack_ref, p_ref, stat_ref, whole_ref, grad_ref,
            *outs[2 * n : 2 * n + 2], total_ref,
        )


def passage_kernel(own_grad_ref, next_grad_ref, own_ref, a_ref, b_ref, out_ref, rows_ref):
    half = a_ref.shape[0]
    rows_ref[:half, :] = a_ref[...]
    rows_ref[half:, :] = b_ref[...]
    for at in range(0, out_ref.shape[1], TILE):
        cols = slice(at, at + TILE)
        out_ref[:, cols] = (
            jnp.dot(own_grad_ref[...], own_ref[:, cols], preferred_element_type=jnp.float32)
            + jnp.dot(next_grad_ref[...], rows_ref[:, cols], preferred_element_type=jnp.float32)
        ).astype(jnp.bfloat16)


def take_kernel(slot, q_ref, out_ref, sem):
    quarter = out_ref.shape[0]
    first = pl.multiple_of((lax.axis_index("grp") ^ slot) * quarter, 16)
    copy = pltpu.make_async_copy(q_ref.at[pl.ds(first, quarter)], out_ref, sem)
    copy.start()
    copy.wait()


def call(kernel, outs, ins, scratch=(), flops=0, name=None, anywhere=0, aliases=None):
    size = sum(math.prod(o.shape) * o.dtype.itemsize for o in list(outs) + list(ins))
    return pl.pallas_call(
        kernel,
        out_shape=tuple(outs),
        input_output_aliases=aliases or {},
        in_specs=[pl.BlockSpec(memory_space=pltpu.HBM)] * anywhere
        + [IN_VMEM] * (len(ins) - anywhere),
        out_specs=(IN_VMEM,) * len(outs),
        scratch_shapes=list(scratch),
        compiler_params=pltpu.CompilerParams(vmem_limit_bytes=24 * 2**20),
        cost_estimate=pl.CostEstimate(
            flops=int(flops), bytes_accessed=int(size), transcendentals=0
        ),
        name=name,
    )(*ins)


def per_device(queries, passages, loss_grad, teacher_logits, passage_ids):
    rows, depth = queries.shape
    width = passages.shape[0]
    quarter, half = rows // 4, rows // 2
    blocks, groups = lax.axis_size("blk"), lax.axis_size("grp")
    blk_index, grp_index = lax.axis_index("blk"), lax.axis_index("grp")
    f32, bf16 = jnp.float32, jnp.bfloat16
    score_scale = 3.0 / math.sqrt(depth)

    def along(by):
        return [
            (b * groups + g, (b + by) % blocks * groups + g)
            for b in range(blocks)
            for g in range(groups)
        ]

    def across(turn):
        return [
            (b * groups + g, b * groups + (g ^ turn))
            for b in range(blocks)
            for g in range(groups)
        ]

    def move(x, pairs):
        return lax.ppermute(x, AXES, pairs)

    stat = shape((8, rows), f32)
    piece = shape((quarter, depth), bf16)
    pack = shape((24, rows), f32)
    scale = score_scale * LOG2E

    def take(slot, name):
        return pl.pallas_call(
            functools.partial(take_kernel, slot),
            out_shape=piece,
            in_specs=[pl.BlockSpec(memory_space=pl.ANY)],
            out_specs=IN_VMEM,
            scratch_shapes=[pltpu.SemaphoreType.DMA(())],
            name=name,
        )(queries)

    a_mine = move(take(0, "take_a"), along(-1))
    b_mine = move(take(2, "take_b"), along(-1))

    exp_own, stat_own, pack_own, pack_out, q_own = call(
        functools.partial(own_kernel, scale, score_scale),
        [shape((width, rows), f32), stat, pack, pack, shape((rows, depth), bf16)],
        [pltpu.with_memory_space_constraint(queries, pltpu.HBM), passages, passage_ids, teacher_logits, loss_grad[None, :]],
        [
            pltpu.SemaphoreType.DMA((4,)),
        ],
        flops=2 * rows * width * depth,
        name="own_scores",
        anywhere=1,
    )
    stat_before = move(stat_own, along(-1))
    a_mine, stat_own = lax.optimization_barrier((a_mine, stat_own))
    a_other = move(a_mine, across(1))

    def next_scores(place, ins, name):
        return call(
            functools.partial(next_kernel, scale, place),
            [shape((width, half), f32), stat, shape((half, depth), bf16)],
            ins,
            flops=2 * half * width * depth,
            name=name,
        )

    exp_a, stat_a, q_a = next_scores(0, [a_mine, a_other, passages], "next_scores_a")
    b_mine, stat_before = lax.optimization_barrier((b_mine, stat_before))
    b_other = move(b_mine, across(1))
    b_mine, pack_out = lax.optimization_barrier((b_mine, pack_out))
    pack_next = move(pack_out, along(-1))
    exp_b, stat_next, q_b = next_scores(
        1, [b_mine, b_other, passages, stat_a, stat_before], "next_scores_b"
    )

    cross, core, both = (move(stat_next, across(turn)) for turn in (2, 1, 3))

    def grads(kernel, ins, count, more, name, aliases=None):
        return call(
            kernel,
            [shape((width, rows), bf16)] + [piece, piece] * count + more,
            [passages] + ins,
            [pltpu.VMEM((half, depth), f32)],
            flops=2 * count * half * width * depth,
            name=name,
            aliases=aliases,
        )

    g_next, nb_mine, nb_other, whole_next = grads(
        first_grad_kernel, [exp_b, pack_next, stat_next, cross, core, both], 1, [stat],
        "next_grad_b",
    )
    nb_in = move(nb_other, across(1))
    nb = (nb_mine.astype(f32) + nb_in.astype(f32)).astype(bf16)
    nb, exp_a, whole_next = lax.optimization_barrier((nb, exp_a, whole_next))
    whole_own = move(whole_next, along(1))
    nb_came = move(nb, along(1))
    g_next, na_mine, na_other = grads(
        functools.partial(grad_kernel, (0,)),
        [exp_a, pack_next, stat_next, whole_next, g_next], 1, [], "next_grad_a", {5: 0},
    )
    of_own = [exp_own, pack_own, stat_own, whole_own]
    g_own, ob_mine, ob_other, oa_mine, oa_other = grads(
        functools.partial(grad_kernel, (1, 0)), of_own, 2, [], "own_grad"
    )
    na_other, ob_other = lax.optimization_barrier((na_other, ob_other))
    na_in = move(na_other, across(1))
    ob_in = move(ob_other, across(1))
    oa_in = move(oa_other, across(1))
    ob_mine, nb_came = lax.optimization_barrier((ob_mine, nb_came))
    ob = (ob_mine.astype(f32) + ob_in.astype(f32) + nb_came.astype(f32)).astype(bf16)
    came_across = move(ob, across(2))
    sent = (na_mine.astype(f32) + na_in.astype(f32)).astype(bf16)
    came_along = move(sent, along(1))
    (passage_grad,) = call(
        passage_kernel,
        [shape((width, depth), bf16)],
        [g_own, g_next, q_own, q_a, q_b],
        [pltpu.VMEM((rows, depth), bf16)],
        flops=4 * rows * width * depth,
        name="passage_grad",
    )
    query_grad = (
        oa_mine.astype(f32)
        + oa_in.astype(f32)
        + came_along.astype(f32)
        + came_across.astype(f32)
    ).astype(bf16)
    return query_grad, passage_grad


def solution(mesh):
    in_specs = (P("blk", None), P(("blk", "grp"), None), P("blk"), P(None, "blk"), P(None, "blk"))
    out_specs = (P(("blk", "grp"), None), P(("blk", "grp"), None))
    return jax.shard_map(
        per_device, mesh=mesh, in_specs=in_specs, out_specs=out_specs, check_vma=False
    )
```

```python
import functools
import math

import jax
import jax.numpy as jnp
from jax import lax
from jax.experimental import pallas as pl
from jax.experimental.pallas import tpu as pltpu
from jax.sharding import PartitionSpec as P

AXES = ("blk", "grp")
LANE = 128
LOG2E = 1.4426950408889634
IN_VMEM = pl.BlockSpec(memory_space=pltpu.VMEM)
TILE = 256
PARTS = 6
STEPS = 3
FEW = 4


def shape(dims, dtype):
    return jax.ShapeDtypeStruct(dims, dtype)


def reorder(x, group):
    half = x.shape[1] // 2
    parts = [x[:, :half], x[:, half:]]
    parts = [jnp.where(group % 2 == 1, pltpu.roll(part, half // 2, 1), part) for part in parts]
    swap = group >= 2
    return jnp.concatenate(
        [jnp.where(swap, parts[1], parts[0]), jnp.where(swap, parts[0], parts[1])], axis=1
    )


def scores(scale, p_ref, q_ref, exp_ref, stat_ref):
    size = p_ref.shape[0] // PARTS
    tops, totals = [], []
    for part in range(PARTS):
        rows = slice(part * size, (part + 1) * size)
        values = scale * lax.dot_general(
            p_ref[rows, :], q_ref[...], (((1,), (1,)), ((), ())),
            preferred_element_type=jnp.float32,
        )
        fold = (size // 8, 8, values.shape[1])
        top = jnp.max(jnp.max(values.reshape(fold), axis=0), axis=0, keepdims=True)
        values = jnp.exp2(values - top)
        exp_ref[rows, :] = values
        total = jnp.sum(jnp.sum(values.reshape(fold), axis=0), axis=0, keepdims=True)
        stat_ref[2 + part : 3 + part, :] = top
        tops.append(top)
        totals.append(total)
    whole = functools.reduce(jnp.maximum, tops)
    stat_ref[0:1, :] = whole
    stat_ref[1:2, :] = sum(total * jnp.exp2(top - whole) for top, total in zip(tops, totals))


def own_kernel(
    scale, coef_scale, q_hbm, p_ref, ids_ref, logits_ref, loss_ref,
    exp_ref, stat_ref, pack_ref, sent_ref, q_ref, sems,
):
    group = lax.axis_index("grp")
    quarter = q_ref.shape[0] // 4
    copies = []
    for slot in range(4):
        first = pl.multiple_of((group ^ slot) * quarter, 16)
        copies.append(
            pltpu.make_async_copy(
                q_hbm.at[pl.ds(first, quarter)],
                q_ref.at[pl.ds(slot * quarter, quarter)],
                sems.at[slot],
            )
        )
    for copy in copies:
        copy.start()
    labels(coef_scale * loss_ref[...], ids_ref, logits_ref, pack_ref, sent_ref, p_ref.shape[0])
    pack_ref[...] = reorder(pack_ref[...], group)
    sent_ref[...] = reorder(sent_ref[...], group)
    for copy in copies:
        copy.wait()
    scores(scale, p_ref, q_ref, exp_ref, stat_ref)


def next_kernel(scale, place, mine_ref, other_ref, p_ref, *refs):
    exp_ref, stat_ref, rows_ref = refs[-3:]
    quarter = mine_ref.shape[0]
    half = 2 * quarter
    rows_ref[:quarter, :] = mine_ref[...]
    rows_ref[quarter:, :] = other_ref[...]
    if place == 1:
        known_ref, before_ref = refs[:2]
        stat_ref[:, :half] = known_ref[:, :half]
    scores(scale, p_ref, rows_ref, exp_ref, stat_ref.at[:, place * half : (place + 1) * half])
    if place == 1:
        top = jnp.maximum(stat_ref[0:1, :], before_ref[0:1, :])
        stat_ref[1:2, :] = stat_ref[1:2, :] * jnp.exp2(stat_ref[0:1, :] - top) + before_ref[
            1:2, :
        ] * jnp.exp2(before_ref[0:1, :] - top)
        stat_ref[0:1, :] = top


def labels(coef, ids_ref, logits_ref, own_ref, next_ref, width):
    device = lax.axis_index("blk") * 4 + lax.axis_index("grp")
    blocks = lax.axis_size("blk")
    before = (lax.axis_index("blk") + blocks - 1) % blocks * 4 + lax.axis_index("grp")
    ids = ids_ref[...]
    logits = logits_ref[...]
    power = jnp.exp(logits - jnp.max(logits, axis=0, keepdims=True))
    weights = coef * (power / jnp.sum(power, axis=0, keepdims=True))
    summed = jnp.zeros_like(weights)
    for k in range(8):
        summed = summed + jnp.where(ids == ids[k : k + 1], weights[k : k + 1], 0.0)
    for ref, at in ((own_ref, device), (next_ref, before)):
        place = ids - at * width
        inside = (place >= 0) & (place < width)
        places, count = [-1.0] * 8, jnp.zeros_like(coef)
        values = [0.0] * 8
        for k in range(8):
            here = inside[k : k + 1]
            for r in range(k + 1):
                chosen = here & (count == r)
                places[r] = jnp.where(chosen, place[k : k + 1].astype(jnp.float32), places[r])
                values[r] = jnp.where(chosen, summed[k : k + 1], values[r])
            count = count + here.astype(jnp.float32)
        for r in range(8):
            ref[r : r + 1, :] = places[r]
            ref[8 + r : 9 + r, :] = values[r]
        ref[16:24, :] = jnp.broadcast_to(coef, ids.shape)


def merge_stats(ref, came, out_ref):
    top = jnp.maximum(ref[0:1, :], came[0:1])
    out_ref[1:2, :] = ref[1:2, :] * jnp.exp2(ref[0:1, :] - top) + came[1:2] * jnp.exp2(
        came[0:1] - top
    )
    out_ref[0:1, :] = top


def chip_stats_kernel(stat_ref, core_ref, out_ref):
    half = core_ref.shape[1] // 2
    core = core_ref[...]
    turned = [pltpu.roll(core[:, at : at + half], half // 2, 1) for at in (0, half)]
    merge_stats(stat_ref, jnp.concatenate(turned, axis=1), out_ref)


def fill_grads(block, count, exp_ref, grad_ref, factor, ids, weights):
    cols = exp_ref.shape[1]
    rows = pl.ds(block * 16, 16)
    place = lax.broadcasted_iota(jnp.int32, (16, cols), 0) + block * 16
    place = place.astype(jnp.float32)
    value = jnp.zeros((16, cols), jnp.float32)
    for k in range(count):
        value = jnp.where(ids[k : k + 1] == place, weights[k : k + 1], value)
    grad_ref[rows, :] = (factor * exp_ref[rows, :] - value).astype(jnp.bfloat16)


def grads_of(
    place, exp_ref, pack_ref, p_ref, stat_ref, whole_ref, grad_ref, mine_ref, other_ref,
    total_ref,
):
    quarter = mine_ref.shape[0]
    lanes = slice(place * 2 * quarter, (place + 1) * 2 * quarter)
    whole = whole_ref[0:2, lanes]
    coef = pack_ref[16:17, lanes] / whole[1:2]
    factors = coef * jnp.exp2(stat_ref[2 : 2 + PARTS, lanes] - whole[0:1])
    ids, weights = pack_ref[0:8, lanes], pack_ref[8:16, lanes]
    exps = exp_ref if exp_ref.shape[1] == 2 * quarter else exp_ref.at[:, lanes]
    grad_ref = grad_ref.at[:, lanes]
    rows = exp_ref.shape[0]
    more = ids[FEW:]
    low = jnp.min(jnp.where(more >= 0, more, float(rows))).astype(jnp.int32) // 16
    high = jnp.max(more).astype(jnp.int32)
    high = jnp.where(high >= 0, high // 16 + 1, 0)
    size = rows // STEPS
    for step in range(STEPS):
        first, last = step * size // 16, (step + 1) * size // 16
        for block in range(first, last):
            part = block * 16 * PARTS // rows
            fill_grads(
                block, FEW, exps, grad_ref, factors[part : part + 1], ids, weights
            )

        def again(block, carry):
            part = block // (rows // PARTS // 16)
            factor = factors[0:1]
            for n in range(1, PARTS):
                factor = jnp.where(part == n, factors[n : n + 1], factor)
            fill_grads(block, 8, exps, grad_ref, factor, ids, weights)
            return carry

        lax.fori_loop(jnp.maximum(low, first), jnp.minimum(high, last), again, 0)
        taken = slice(step * size, (step + 1) * size)
        for at in range(0, p_ref.shape[1], TILE):
            cols = slice(at, at + TILE)
            part = lax.dot_general(
                grad_ref[taken, :], p_ref[taken, cols], (((0,), (0,)), ((), ())),
                preferred_element_type=jnp.float32,
            )
            if step > 0:
                part = total_ref[:, cols] + part
            if step < STEPS - 1:
                total_ref[:, cols] = part
            else:
                mine_ref[:, cols] = part[:quarter].astype(jnp.bfloat16)
                other_ref[:, cols] = part[quarter:].astype(jnp.bfloat16)


def first_grad_kernel(p_ref, exp_ref, pack_ref, stat_ref, chip_ref, cross_ref, *outs):
    *outs, whole_ref, total_ref = outs
    half = cross_ref.shape[1] // 2
    cross = cross_ref[...]
    merge_stats(
        chip_ref, jnp.concatenate([cross[:, half:], cross[:, :half]], axis=1), whole_ref
    )
    grads_of(1, exp_ref, pack_ref, p_ref, stat_ref, whole_ref, *outs, total_ref)


def grad_kernel(places, p_ref, *refs):
    exp_ref, pack_ref, stat_ref, whole_ref = refs[:4]
    grad_ref, *outs, total_ref = refs[-2 - 2 * len(places) :]
    for n, place in enumerate(places):
        grads_of(
            place, exp_ref, pack_ref, p_ref, stat_ref, whole_ref, grad_ref,
            *outs[2 * n : 2 * n + 2], total_ref,
        )


def passage_kernel(own_grad_ref, next_grad_ref, own_ref, a_ref, b_ref, out_ref, rows_ref):
    half = a_ref.shape[0]
    rows_ref[:half, :] = a_ref[...]
    rows_ref[half:, :] = b_ref[...]
    for at in range(0, out_ref.shape[1], TILE):
        cols = slice(at, at + TILE)
        out_ref[:, cols] = (
            jnp.dot(own_grad_ref[...], own_ref[:, cols], preferred_element_type=jnp.float32)
            + jnp.dot(next_grad_ref[...], rows_ref[:, cols], preferred_element_type=jnp.float32)
        ).astype(jnp.bfloat16)


def take_kernel(slot, q_ref, out_ref, sem):
    quarter = out_ref.shape[0]
    first = pl.multiple_of((lax.axis_index("grp") ^ slot) * quarter, 16)
    copy = pltpu.make_async_copy(q_ref.at[pl.ds(first, quarter)], out_ref, sem)
    copy.start()
    copy.wait()


def call(kernel, outs, ins, scratch=(), flops=0, name=None, anywhere=0, aliases=None):
    size = sum(math.prod(o.shape) * o.dtype.itemsize for o in list(outs) + list(ins))
    return pl.pallas_call(
        kernel,
        out_shape=tuple(outs),
        input_output_aliases=aliases or {},
        in_specs=[pl.BlockSpec(memory_space=pltpu.HBM)] * anywhere
        + [IN_VMEM] * (len(ins) - anywhere),
        out_specs=(IN_VMEM,) * len(outs),
        scratch_shapes=list(scratch),
        compiler_params=pltpu.CompilerParams(vmem_limit_bytes=24 * 2**20),
        cost_estimate=pl.CostEstimate(
            flops=int(flops), bytes_accessed=int(size), transcendentals=0
        ),
        name=name,
    )(*ins)


def per_device(queries, passages, loss_grad, teacher_logits, passage_ids):
    rows, depth = queries.shape
    width = passages.shape[0]
    quarter, half = rows // 4, rows // 2
    blocks, groups = lax.axis_size("blk"), lax.axis_size("grp")
    blk_index, grp_index = lax.axis_index("blk"), lax.axis_index("grp")
    f32, bf16 = jnp.float32, jnp.bfloat16
    score_scale = 3.0 / math.sqrt(depth)

    def along(by):
        return [
            (b * groups + g, (b + by) % blocks * groups + g)
            for b in range(blocks)
            for g in range(groups)
        ]

    def across(turn):
        return [
            (b * groups + g, b * groups + (g ^ turn))
            for b in range(blocks)
            for g in range(groups)
        ]

    def move(x, pairs):
        return lax.ppermute(x, AXES, pairs)

    stat = shape((8, rows), f32)
    piece = shape((quarter, depth), bf16)
    pack = shape((24, rows), f32)
    scale = score_scale * LOG2E

    def take(slot, name):
        return pl.pallas_call(
            functools.partial(take_kernel, slot),
            out_shape=piece,
            in_specs=[pl.BlockSpec(memory_space=pl.ANY)],
            out_specs=IN_VMEM,
            scratch_shapes=[pltpu.SemaphoreType.DMA(())],
            name=name,
        )(queries)

    a_mine = move(take(0, "take_a"), along(-1))
    b_mine = move(take(2, "take_b"), along(-1))

    exp_own, stat_own, pack_own, pack_out, q_own = call(
        functools.partial(own_kernel, scale, score_scale),
        [shape((width, rows), f32), stat, pack, pack, shape((rows, depth), bf16)],
        [pltpu.with_memory_space_constraint(queries, pltpu.HBM), passages, passage_ids, teacher_logits, loss_grad[None, :]],
        [
            pltpu.SemaphoreType.DMA((4,)),
        ],
        flops=2 * rows * width * depth,
        name="own_scores",
        anywhere=1,
    )
    stat_before = move(stat_own, along(-1))
    a_mine, stat_own = lax.optimization_barrier((a_mine, stat_own))
    a_other = move(a_mine, across(1))

    def next_scores(place, ins, name):
        return call(
            functools.partial(next_kernel, scale, place),
            [shape((width, half), f32), stat, shape((half, depth), bf16)],
            ins,
            flops=2 * half * width * depth,
            name=name,
        )

    exp_a, stat_a, q_a = next_scores(0, [a_mine, a_other, passages], "next_scores_a")
    b_mine, stat_before = lax.optimization_barrier((b_mine, stat_before))
    b_other = move(b_mine, across(1))
    b_mine, pack_out = lax.optimization_barrier((b_mine, pack_out))
    pack_next = move(pack_out, along(-1))
    exp_b, stat_next, q_b = next_scores(
        1, [b_mine, b_other, passages, stat_a, stat_before], "next_scores_b"
    )

    (stat_chip,) = call(
        chip_stats_kernel, [stat], [stat_next, move(stat_next, across(1))], name="chip_stats"
    )
    cross = move(stat_chip, across(2))

    def grads(kernel, ins, count, more, name, aliases=None):
        return call(
            kernel,
            [shape((width, rows), bf16)] + [piece, piece] * count + more,
            [passages] + ins,
            [pltpu.VMEM((half, depth), f32)],
            flops=2 * count * half * width * depth,
            name=name,
            aliases=aliases,
        )

    g_next, nb_mine, nb_other, whole_next = grads(
        first_grad_kernel, [exp_b, pack_next, stat_next, stat_chip, cross], 1, [stat],
        "next_grad_b",
    )
    nb_in = move(nb_other, across(1))
    nb = (nb_mine.astype(f32) + nb_in.astype(f32)).astype(bf16)
    nb, exp_a, whole_next = lax.optimization_barrier((nb, exp_a, whole_next))
    whole_own = move(whole_next, along(1))
    nb_came = move(nb, along(1))
    g_next, na_mine, na_other = grads(
        functools.partial(grad_kernel, (0,)),
        [exp_a, pack_next, stat_next, whole_next, g_next], 1, [], "next_grad_a", {5: 0},
    )
    of_own = [exp_own, pack_own, stat_own, whole_own]
    g_own, ob_mine, ob_other, oa_mine, oa_other = grads(
        functools.partial(grad_kernel, (1, 0)), of_own, 2, [], "own_grad"
    )
    na_other, ob_other = lax.optimization_barrier((na_other, ob_other))
    na_in = move(na_other, across(1))
    ob_in = move(ob_other, across(1))
    oa_in = move(oa_other, across(1))
    ob_mine, nb_came = lax.optimization_barrier((ob_mine, nb_came))
    ob = (ob_mine.astype(f32) + ob_in.astype(f32) + nb_came.astype(f32)).astype(bf16)
    came_across = move(ob, across(2))
    ob, na_in = lax.optimization_barrier((ob, na_in))
    sent = (na_mine.astype(f32) + na_in.astype(f32)).astype(bf16)
    came_along = move(sent, along(1))
    (passage_grad,) = call(
        passage_kernel,
        [shape((width, depth), bf16)],
        [g_own, g_next, q_own, q_a, q_b],
        [pltpu.VMEM((rows, depth), bf16)],
        flops=4 * rows * width * depth,
        name="passage_grad",
    )
    query_grad = (
        oa_mine.astype(f32)
        + oa_in.astype(f32)
        + came_along.astype(f32)
        + came_across.astype(f32)
    ).astype(bf16)
    return query_grad, passage_grad


def solution(mesh):
    in_specs = (P("blk", None), P(("blk", "grp"), None), P("blk"), P(None, "blk"), P(None, "blk"))
    out_specs = (P(("blk", "grp"), None), P(("blk", "grp"), None))
    return jax.shard_map(
        per_device, mesh=mesh, in_specs=in_specs, out_specs=out_specs, check_vma=False
    )
```

```python
import functools
import math

import jax
import jax.numpy as jnp
from jax import lax
from jax.experimental import pallas as pl
from jax.experimental.pallas import tpu as pltpu
from jax.sharding import PartitionSpec as P

AXES = ("blk", "grp")
LANE = 128
LOG2E = 1.4426950408889634
IN_VMEM = pl.BlockSpec(memory_space=pltpu.VMEM)
TILE = 256
PARTS = 6
STEPS = 3
FEW = 4


def shape(dims, dtype):
    return jax.ShapeDtypeStruct(dims, dtype)


def reorder(x, group):
    half = x.shape[1] // 2
    parts = [x[:, :half], x[:, half:]]
    parts = [jnp.where(group % 2 == 1, pltpu.roll(part, half // 2, 1), part) for part in parts]
    swap = group >= 2
    return jnp.concatenate(
        [jnp.where(swap, parts[1], parts[0]), jnp.where(swap, parts[0], parts[1])], axis=1
    )


def scores(scale, p_ref, q_ref, exp_ref, stat_ref):
    size = p_ref.shape[0] // PARTS
    tops, totals = [], []
    for part in range(PARTS):
        rows = slice(part * size, (part + 1) * size)
        values = scale * lax.dot_general(
            p_ref[rows, :], q_ref[...], (((1,), (1,)), ((), ())),
            preferred_element_type=jnp.float32,
        )
        fold = (size // 8, 8, values.shape[1])
        top = jnp.max(jnp.max(values.reshape(fold), axis=0), axis=0, keepdims=True)
        values = jnp.exp2(values - top)
        exp_ref[rows, :] = values
        total = jnp.sum(jnp.sum(values.reshape(fold), axis=0), axis=0, keepdims=True)
        stat_ref[2 + part : 3 + part, :] = top
        tops.append(top)
        totals.append(total)
    whole = functools.reduce(jnp.maximum, tops)
    stat_ref[0:1, :] = whole
    stat_ref[1:2, :] = sum(total * jnp.exp2(top - whole) for top, total in zip(tops, totals))


def own_kernel(
    scale, coef_scale, q_hbm, p_ref, ids_ref, logits_ref, loss_ref,
    exp_ref, stat_ref, pack_ref, sent_ref, q_ref, sems,
):
    group = lax.axis_index("grp")
    quarter = q_ref.shape[0] // 4
    copies = []
    for slot in range(4):
        first = pl.multiple_of((group ^ slot) * quarter, 16)
        copies.append(
            pltpu.make_async_copy(
                q_hbm.at[pl.ds(first, quarter)],
                q_ref.at[pl.ds(slot * quarter, quarter)],
                sems.at[slot],
            )
        )
    for copy in copies:
        copy.start()
    labels(coef_scale * loss_ref[...], ids_ref, logits_ref, pack_ref, sent_ref, p_ref.shape[0])
    pack_ref[...] = reorder(pack_ref[...], group)
    sent_ref[...] = reorder(sent_ref[...], group)
    for copy in copies:
        copy.wait()
    scores(scale, p_ref, q_ref, exp_ref, stat_ref)


def next_kernel(scale, place, mine_ref, other_ref, p_ref, *refs):
    exp_ref, stat_ref, rows_ref = refs[-3:]
    quarter = mine_ref.shape[0]
    half = 2 * quarter
    rows_ref[:quarter, :] = mine_ref[...]
    rows_ref[quarter:, :] = other_ref[...]
    if place == 1:
        known_ref, before_ref = refs[:2]
        stat_ref[:, :half] = known_ref[:, :half]
    scores(scale, p_ref, rows_ref, exp_ref, stat_ref.at[:, place * half : (place + 1) * half])
    if place == 1:
        top = jnp.maximum(stat_ref[0:1, :], before_ref[0:1, :])
        stat_ref[1:2, :] = stat_ref[1:2, :] * jnp.exp2(stat_ref[0:1, :] - top) + before_ref[
            1:2, :
        ] * jnp.exp2(before_ref[0:1, :] - top)
        stat_ref[0:1, :] = top


def labels(coef, ids_ref, logits_ref, own_ref, next_ref, width):
    device = lax.axis_index("blk") * 4 + lax.axis_index("grp")
    blocks = lax.axis_size("blk")
    before = (lax.axis_index("blk") + blocks - 1) % blocks * 4 + lax.axis_index("grp")
    ids = ids_ref[...]
    logits = logits_ref[...]
    power = jnp.exp(logits - jnp.max(logits, axis=0, keepdims=True))
    weights = coef * (power / jnp.sum(power, axis=0, keepdims=True))
    summed = jnp.zeros_like(weights)
    for k in range(8):
        summed = summed + jnp.where(ids == ids[k : k + 1], weights[k : k + 1], 0.0)
    for ref, at in ((own_ref, device), (next_ref, before)):
        place = ids - at * width
        inside = (place >= 0) & (place < width)
        places, count = [-1.0] * 8, jnp.zeros_like(coef)
        values = [0.0] * 8
        for k in range(8):
            here = inside[k : k + 1]
            for r in range(k + 1):
                chosen = here & (count == r)
                places[r] = jnp.where(chosen, place[k : k + 1].astype(jnp.float32), places[r])
                values[r] = jnp.where(chosen, summed[k : k + 1], values[r])
            count = count + here.astype(jnp.float32)
        for r in range(8):
            ref[r : r + 1, :] = places[r]
            ref[8 + r : 9 + r, :] = values[r]
        ref[16:24, :] = jnp.broadcast_to(coef, ids.shape)


def merge_stats(ref, came, out_ref):
    top = jnp.maximum(ref[0:1, :], came[0:1])
    out_ref[1:2, :] = ref[1:2, :] * jnp.exp2(ref[0:1, :] - top) + came[1:2] * jnp.exp2(
        came[0:1] - top
    )
    out_ref[0:1, :] = top


def chip_stats_kernel(stat_ref, core_ref, out_ref):
    half = core_ref.shape[1] // 2
    core = core_ref[...]
    turned = [pltpu.roll(core[:, at : at + half], half // 2, 1) for at in (0, half)]
    merge_stats(stat_ref, jnp.concatenate(turned, axis=1), out_ref)


def fill_grads(block, count, exp_ref, grad_ref, factor, ids, weights):
    cols = exp_ref.shape[1]
    rows = pl.ds(block * 16, 16)
    place = lax.broadcasted_iota(jnp.int32, (16, cols), 0) + block * 16
    place = place.astype(jnp.float32)
    value = jnp.zeros((16, cols), jnp.float32)
    for k in range(count):
        value = jnp.where(ids[k : k + 1] == place, weights[k : k + 1], value)
    grad_ref[rows, :] = (factor * exp_ref[rows, :] - value).astype(jnp.bfloat16)


def grads_of(
    place, exp_ref, pack_ref, p_ref, stat_ref, whole_ref, grad_ref, mine_ref, other_ref,
    total_ref,
):
    quarter = mine_ref.shape[0]
    lanes = slice(place * 2 * quarter, (place + 1) * 2 * quarter)
    whole = whole_ref[0:2, lanes]
    coef = pack_ref[16:17, lanes] / whole[1:2]
    factors = coef * jnp.exp2(stat_ref[2 : 2 + PARTS, lanes] - whole[0:1])
    ids, weights = pack_ref[0:8, lanes], pack_ref[8:16, lanes]
    exps = exp_ref if exp_ref.shape[1] == 2 * quarter else exp_ref.at[:, lanes]
    grad_ref = grad_ref.at[:, lanes]
    rows = exp_ref.shape[0]
    more = ids[FEW:]
    low = jnp.min(jnp.where(more >= 0, more, float(rows))).astype(jnp.int32) // 16
    high = jnp.max(more).astype(jnp.int32)
    high = jnp.where(high >= 0, high // 16 + 1, 0)
    size = rows // STEPS
    for step in range(STEPS):
        first, last = step * size // 16, (step + 1) * size // 16
        for block in range(first, last):
            part = block * 16 * PARTS // rows
            fill_grads(
                block, FEW, exps, grad_ref, factors[part : part + 1], ids, weights
            )

        def again(block, carry):
            part = block // (rows // PARTS // 16)
            factor = factors[0:1]
            for n in range(1, PARTS):
                factor = jnp.where(part == n, factors[n : n + 1], factor)
            fill_grads(block, 8, exps, grad_ref, factor, ids, weights)
            return carry

        lax.fori_loop(jnp.maximum(low, first), jnp.minimum(high, last), again, 0)
        taken = slice(step * size, (step + 1) * size)
        for at in range(0, p_ref.shape[1], TILE):
            cols = slice(at, at + TILE)
            part = lax.dot_general(
                grad_ref[taken, :], p_ref[taken, cols], (((0,), (0,)), ((), ())),
                preferred_element_type=jnp.float32,
            )
            if step > 0:
                part = total_ref[:, cols] + part
            if step < STEPS - 1:
                total_ref[:, cols] = part
            else:
                mine_ref[:, cols] = part[:quarter].astype(jnp.bfloat16)
                other_ref[:, cols] = part[quarter:].astype(jnp.bfloat16)


def first_grad_kernel(p_ref, exp_ref, pack_ref, stat_ref, chip_ref, cross_ref, *outs):
    *outs, whole_ref, total_ref = outs
    half = cross_ref.shape[1] // 2
    cross = cross_ref[...]
    merge_stats(
        chip_ref, jnp.concatenate([cross[:, half:], cross[:, :half]], axis=1), whole_ref
    )
    grads_of(1, exp_ref, pack_ref, p_ref, stat_ref, whole_ref, *outs, total_ref)


def grad_kernel(places, p_ref, *refs):
    exp_ref, pack_ref, stat_ref, whole_ref = refs[:4]
    grad_ref, *outs, total_ref = refs[-2 - 2 * len(places) :]
    for n, place in enumerate(places):
        grads_of(
            place, exp_ref, pack_ref, p_ref, stat_ref, whole_ref, grad_ref,
            *outs[2 * n : 2 * n + 2], total_ref,
        )


def passage_kernel(own_grad_ref, next_grad_ref, own_ref, a_ref, b_ref, out_ref, rows_ref):
    half = a_ref.shape[0]
    rows_ref[:half, :] = a_ref[...]
    rows_ref[half:, :] = b_ref[...]
    for at in range(0, out_ref.shape[1], TILE):
        cols = slice(at, at + TILE)
        out_ref[:, cols] = (
            jnp.dot(own_grad_ref[...], own_ref[:, cols], preferred_element_type=jnp.float32)
            + jnp.dot(next_grad_ref[...], rows_ref[:, cols], preferred_element_type=jnp.float32)
        ).astype(jnp.bfloat16)


def take_kernel(slot, q_ref, out_ref, sem):
    quarter = out_ref.shape[0]
    first = pl.multiple_of((lax.axis_index("grp") ^ slot) * quarter, 16)
    copy = pltpu.make_async_copy(q_ref.at[pl.ds(first, quarter)], out_ref, sem)
    copy.start()
    copy.wait()


def call(kernel, outs, ins, scratch=(), flops=0, name=None, anywhere=0, aliases=None):
    size = sum(math.prod(o.shape) * o.dtype.itemsize for o in list(outs) + list(ins))
    return pl.pallas_call(
        kernel,
        out_shape=tuple(outs),
        input_output_aliases=aliases or {},
        in_specs=[pl.BlockSpec(memory_space=pltpu.HBM)] * anywhere
        + [IN_VMEM] * (len(ins) - anywhere),
        out_specs=(IN_VMEM,) * len(outs),
        scratch_shapes=list(scratch),
        compiler_params=pltpu.CompilerParams(vmem_limit_bytes=24 * 2**20),
        cost_estimate=pl.CostEstimate(
            flops=int(flops), bytes_accessed=int(size), transcendentals=0
        ),
        name=name,
    )(*ins)


def per_device(queries, passages, loss_grad, teacher_logits, passage_ids):
    rows, depth = queries.shape
    width = passages.shape[0]
    quarter, half = rows // 4, rows // 2
    blocks, groups = lax.axis_size("blk"), lax.axis_size("grp")
    blk_index, grp_index = lax.axis_index("blk"), lax.axis_index("grp")
    f32, bf16 = jnp.float32, jnp.bfloat16
    score_scale = 3.0 / math.sqrt(depth)

    def along(by):
        return [
            (b * groups + g, (b + by) % blocks * groups + g)
            for b in range(blocks)
            for g in range(groups)
        ]

    def across(turn):
        return [
            (b * groups + g, b * groups + (g ^ turn))
            for b in range(blocks)
            for g in range(groups)
        ]

    def move(x, pairs):
        return lax.ppermute(x, AXES, pairs)

    stat = shape((8, rows), f32)
    piece = shape((quarter, depth), bf16)
    pack = shape((24, rows), f32)
    scale = score_scale * LOG2E

    def take(slot, name):
        return pl.pallas_call(
            functools.partial(take_kernel, slot),
            out_shape=piece,
            in_specs=[pl.BlockSpec(memory_space=pl.ANY)],
            out_specs=IN_VMEM,
            scratch_shapes=[pltpu.SemaphoreType.DMA(())],
            name=name,
        )(queries)

    a_mine = move(take(0, "take_a"), along(-1))
    b_mine = move(take(2, "take_b"), along(-1))

    exp_own, stat_own, pack_own, pack_out, q_own = call(
        functools.partial(own_kernel, scale, score_scale),
        [shape((width, rows), f32), stat, pack, pack, shape((rows, depth), bf16)],
        [pltpu.with_memory_space_constraint(queries, pltpu.HBM), passages, passage_ids, teacher_logits, loss_grad[None, :]],
        [
            pltpu.SemaphoreType.DMA((4,)),
        ],
        flops=2 * rows * width * depth,
        name="own_scores",
        anywhere=1,
    )
    stat_before = move(stat_own, along(-1))
    a_mine, stat_own = lax.optimization_barrier((a_mine, stat_own))
    a_other = move(a_mine, across(1))

    def next_scores(place, ins, name):
        return call(
            functools.partial(next_kernel, scale, place),
            [shape((width, half), f32), stat, shape((half, depth), bf16)],
            ins,
            flops=2 * half * width * depth,
            name=name,
        )

    exp_a, stat_a, q_a = next_scores(0, [a_mine, a_other, passages], "next_scores_a")
    b_mine, stat_before = lax.optimization_barrier((b_mine, stat_before))
    b_other = move(b_mine, across(1))
    b_mine, pack_out = lax.optimization_barrier((b_mine, pack_out))
    pack_next = move(pack_out, along(-1))
    exp_b, stat_next, q_b = next_scores(
        1, [b_mine, b_other, passages, stat_a, stat_before], "next_scores_b"
    )

    (stat_chip,) = call(
        chip_stats_kernel, [stat], [stat_next, move(stat_next, across(1))], name="chip_stats"
    )
    cross = move(stat_chip, across(2))

    def grads(kernel, ins, count, more, name, aliases=None):
        return call(
            kernel,
            [shape((width, rows), bf16)] + [piece, piece] * count + more,
            [passages] + ins,
            [pltpu.VMEM((half, depth), f32)],
            flops=2 * count * half * width * depth,
            name=name,
            aliases=aliases,
        )

    g_next, nb_mine, nb_other, whole_next = grads(
        first_grad_kernel, [exp_b, pack_next, stat_next, stat_chip, cross], 1, [stat],
        "next_grad_b",
    )
    nb_in = move(nb_other, across(1))
    nb = (nb_mine.astype(f32) + nb_in.astype(f32)).astype(bf16)
    nb, exp_a, whole_next = lax.optimization_barrier((nb, exp_a, whole_next))
    whole_own = move(whole_next, along(1))
    nb_came = move(nb, along(1))
    g_next, na_mine, na_other = grads(
        functools.partial(grad_kernel, (0,)),
        [exp_a, pack_next, stat_next, whole_next, g_next], 1, [], "next_grad_a", {5: 0},
    )
    of_own = [exp_own, pack_own, stat_own, whole_own]
    g_own, ob_mine, ob_other, oa_mine, oa_other = grads(
        functools.partial(grad_kernel, (1, 0)), of_own, 2, [], "own_grad"
    )
    na_other, ob_other = lax.optimization_barrier((na_other, ob_other))
    na_in = move(na_other, across(1))
    ob_in = move(ob_other, across(1))
    oa_in = move(oa_other, across(1))
    ob_mine, nb_came = lax.optimization_barrier((ob_mine, nb_came))
    ob = (ob_mine.astype(f32) + ob_in.astype(f32) + nb_came.astype(f32)).astype(bf16)
    came_across = move(ob, across(2))
    sent = (na_mine.astype(f32) + na_in.astype(f32)).astype(bf16)
    came_along = move(sent, along(1))
    (passage_grad,) = call(
        passage_kernel,
        [shape((width, depth), bf16)],
        [g_own, g_next, q_own, q_a, q_b],
        [pltpu.VMEM((rows, depth), bf16)],
        flops=4 * rows * width * depth,
        name="passage_grad",
    )
    query_grad = (
        oa_mine.astype(f32)
        + oa_in.astype(f32)
        + came_along.astype(f32)
        + came_across.astype(f32)
    ).astype(bf16)
    return query_grad, passage_grad


def solution(mesh):
    in_specs = (P("blk", None), P(("blk", "grp"), None), P("blk"), P(None, "blk"), P(None, "blk"))
    out_specs = (P(("blk", "grp"), None), P(("blk", "grp"), None))
    return jax.shard_map(
        per_device, mesh=mesh, in_specs=in_specs, out_specs=out_specs, check_vma=False
    )
```
